256 devices in a mesh: azim: 32 (over z, x), rad: 4 (over y_hi, core), group: 2 (over y_lo).
Axes of the slice: x: 4, y: 4 (y_hi: 2, y_lo: 2; y = y_hi * 2 + y_lo), z: 8, core: 2. Of those that a mesh axis runs over, the one named last changes fastest.
Arguments:
- les_state: float32 [5, 320, 40, 1280], P(None, 'azim', 'rad', 'group'), may hold values from -1 to 6, as said below
- acoustic_state: float32 [4, 160, 20, 1280], P(None, 'azim', 'rad', 'group'), may hold values from -6 to 6
- mean_density: float32 [160, 20, 1280], P('azim', 'rad', 'group'), may hold values from 0.8 to 1.25
- mean_sound: float32 [160, 20, 1280], P('azim', 'rad', 'group'), may hold values from 0.8 to 1.2
- mean_velocity: float32 [3, 160, 20, 1280], P(None, 'azim', 'rad', 'group'), may hold values from -0.4 to 0.4
- projection: float32 [8, 125, 125], replicated, may hold values from -0.5 to 0.5
- intersection_counts: int32 [32, 4, 2, 128], P('azim', 'rad', 'group'), may hold values from 1 to 16, 768 in all within a row
- intersection_elem: int32 [32, 4, 2, 768], P('azim', 'rad', 'group'), may hold values from 0 to 767
- intersection_pattern: int32 [32, 4, 2, 768], P('azim', 'rad', 'group'), may hold values from 0 to 7
Outputs:
- les_next: float32 [5, 320, 40, 1280], P(None, 'azim', 'rad', 'group')
- acoustic_next: float32 [4, 160, 20, 1280], P(None, 'azim', 'rad', 'group')
The draws below stay inside these ranges and needn't reach their ends.
Inputs may be any that keep to these rules, and one draw needn't show every extreme that they name: `les_state`: density lies in 0.7 to 1.4 and pressure 0.4 (E - |m|^2 / (2 rho)) in 0.5 to 2 at every node. `intersection_counts`: the counts of one block sum to 768.
All inputs are finite; a program needn't handle non-finite values.
Results may differ from the reference program's by a relative error of at most 0.0003.
Values sent between devices are 32-bit elements; how exact they have to be, the bound alone decides.
No kernel may reach another device: no remote copies, remote signals or barrier semaphores. Data moves between devices by JAX's collectives and lax.ppermute only.
A program may use at most 128 MiB of HBM per device.

```python
import math
from functools import partial
import jax
import jax.numpy as jnp
import numpy as np
from jax import lax

EA = 2
ER = 2
EX = 128
PAT = 8
MOST = 16
EL = 512
COL = 256
AA = 1
AR = 1
AEL = 128
OVL = 768
SECTORS = 32
RBLOCKS = 4
HALVES = 2
NAG = 320
NRG = 40
NXG = 1280
ANAG = 160
ANRG = 20
ANXG = 1280
N_AZIM = 32
N_RAD = 4
N_GROUP = 2


def draw_les_state(key, part):
    key = jax.random.fold_in(key, 11)
    subkeys = jax.random.split(key, 3)
    extent = (NAG, NRG, NXG)
    density = jax.random.uniform(subkeys[0], extent, jnp.float32, 0.8, 1.25)
    velocity = jax.random.uniform(subkeys[1], (3,) + extent, jnp.float32, -0.5, 0.5)
    pressure = jax.random.uniform(subkeys[2], extent, jnp.float32, 0.6, 1.6)
    momentum = density[None] * velocity
    energy = pressure / 0.4 + 0.5 * density * jnp.sum(velocity * velocity, axis=0)
    return jnp.concatenate([density[None], momentum, energy[None]], axis=0)


def set_ends(entries, stream_key, least, top_value):
    longest = entries.shape.index(max(entries.shape))
    spots = []
    for shift in (0, 1):
        where = [jax.random.randint(jax.random.fold_in(stream_key, axis), (), 0, length) for axis, length in enumerate(entries.shape)]
        where[longest] = (where[longest] + shift) % entries.shape[longest]
        spots.append(tuple(where))
    return entries.at[spots[0]].set(least).at[spots[1]].set(top_value)


def block_scale(key, dims, cuts, least, largest):
    def one(dim, parts):
        heights = jax.random.uniform(jax.random.fold_in(jax.random.fold_in(key, 6), dim), (parts,), jnp.float32, least / len(cuts), largest / len(cuts))
        return jnp.repeat(jnp.exp(heights), dims[dim] // parts).reshape((-1,) + (1,) * (len(dims) - dim - 1))

    loudness = one(*cuts[0])
    for cut in cuts[1:]:
        loudness = loudness * one(*cut)
    return loudness


def profile(number_of, total, reach, lean):
    portions = [(1 << 20) // math.isqrt(grade ** lean) + 1 for grade in range(2, number_of + 1)]
    surplus, counts = total - reach - (number_of - 1), [1] * (number_of - 1)
    while surplus > 0:
        free = [i for i in range(number_of - 1) if counts[i] < reach]
        mass, left = sum([portions[i] for i in free]), surplus
        for i in free:
            addition = min(reach - counts[i], max(1, left * portions[i] // mass), surplus)
            counts[i] = counts[i] + addition
            surplus = surplus - addition
    return np.array([reach] + counts)


def uneven(key, amount, total, most, skew):
    if amount == 2:
        one = jax.random.randint(key, (), max(1, total - most), min(most, total - 1) + 1)
        return jnp.stack([one, total - one])
    tallies = jnp.asarray(profile(amount, total, most, skew), jnp.int32)
    twos = (amount - 1) // 2
    source_of, taker = tallies[1:1 + 2 * twos:2], tallies[2:2 + 2 * twos:2]
    margin = jnp.minimum(source_of - 1, most - taker)
    shifted = jax.random.randint(jax.random.fold_in(key, 1), (twos,), 0, 1 << 20) % (margin + 1)
    tallies = tallies.at[1:1 + 2 * twos:2].set(source_of - shifted).at[2:2 + 2 * twos:2].set(taker + shifted)
    return tallies[jax.random.permutation(jax.random.fold_in(key, 2), amount)]


def scatter_about(rng, dims, scale, bound, cuts=(), kind=jnp.bfloat16):
    drawn = scale * jax.random.normal(rng, dims, jnp.float32)
    if cuts:
        drawn = drawn * block_scale(rng, dims, cuts, -0.22, 0.18)
    return jnp.clip(drawn, -bound, bound).astype(kind)


def setup_inputs(seed: int = 0) -> dict:
    keys = jax.random.split(jax.random.key(seed), 10)
    return {
        "les_state": draw_les_state(jax.random.fold_in(keys[9], 71), 0),
        "acoustic_state": scatter_about(keys[1], (4, ANAG, ANRG, ANXG), 1.0, 6.0, ((1, 32), (2, 4), (3, 2)), jnp.float32),
        "mean_density": jnp.clip(0.8 + 0.45 * jax.random.uniform(keys[2], (ANAG, ANRG, ANXG), jnp.float32) ** block_scale(keys[2], (ANAG, ANRG, ANXG), ((0, 32), (1, 4), (2, 2)), -0.2, 0.2), 0.8, 1.25),
        "mean_sound": jnp.clip(0.8 + 0.40000004 * jax.random.uniform(keys[3], (ANAG, ANRG, ANXG), jnp.float32) ** block_scale(keys[3], (ANAG, ANRG, ANXG), ((0, 32), (1, 4), (2, 2)), -0.2, 0.2), 0.8, 1.2),
        "mean_velocity": jnp.clip(jax.random.uniform(keys[4], (3, ANAG, ANRG, ANXG), jnp.float32, -0.4, 0.4) * block_scale(keys[4], (3, ANAG, ANRG, ANXG), ((1, 32), (2, 4), (3, 2)), -0.4, 0.0), -0.4, 0.4),
        "projection": scatter_about(keys[5], (PAT, 125, 125), 125 ** -0.5, 0.5, (), jnp.float32),
        "intersection_counts": jax.vmap(lambda own: uneven(own, AEL, OVL, MOST, 2))(jax.random.split(keys[6], SECTORS * RBLOCKS * HALVES)).reshape((SECTORS, RBLOCKS, HALVES, AEL)).astype(jnp.int32),
        "intersection_elem": set_ends(jax.random.randint(keys[7], (SECTORS, RBLOCKS, HALVES, OVL), 0, EL + COL), jax.random.fold_in(keys[7], 1), 0, (EL + COL) - 1).astype(jnp.int32),
        "intersection_pattern": set_ends(jax.random.randint(keys[8], (SECTORS, RBLOCKS, HALVES, OVL), 0, PAT), jax.random.fold_in(keys[8], 1), 0, PAT - 1).astype(jnp.int32),
    }


HEAT_RATIO = 1.4
TIME_STEP = 0.05
EDGE_WEIGHT = 0.1

def gll_derivative():
    points = np.array([-1.0, -math.sqrt(3.0 / 7.0), 0.0, math.sqrt(3.0 / 7.0), 1.0])
    barycentric = np.array([1.0 / np.prod([points[j] - points[k] for k in range(5) if k != j]) for j in range(5)])
    matrix = np.zeros((5, 5))
    for i in range(5):
        for j in range(5):
            if i != j:
                matrix[i, j] = barycentric[j] / barycentric[i] / (points[i] - points[j])
        matrix[i, i] = -np.sum(matrix[i])
    return jnp.asarray(matrix, jnp.float32)

def along_axis(values, matrix, axis_dim):
    extent = values.shape
    blocks = values.reshape(extent[:axis_dim] + (extent[axis_dim] // 5, 5) + extent[axis_dim + 1:])
    letters = 'abcdefg'[:blocks.ndim]
    summed_letter = letters[axis_dim + 1]
    formula = letters + ',z' + summed_letter + '->' + letters.replace(summed_letter, 'z')
    result = jnp.einsum(formula, blocks, matrix, precision=lax.Precision.HIGHEST)
    return result.reshape(extent)

def line_term(interior, extended, flux_of, speed_of, solved, axis_dim, derivative):
    volume = along_axis(flux_of(interior), derivative, axis_dim)
    length = extended.shape[axis_dim]
    elements = (length - 2) // 5
    left_state = lax.slice_in_dim(extended, 0, length - 1, 5, axis_dim)
    right_state = lax.slice_in_dim(extended, 1, length, 5, axis_dim)
    flux_left = flux_of(left_state)
    flux_right = flux_of(right_state)
    wave_speed = jnp.maximum(speed_of(left_state), speed_of(right_state))
    state_jump = lax.slice_in_dim(right_state - left_state, 0, solved, 1, 0)
    common = 0.5 * (flux_left + flux_right) - 0.5 * wave_speed[None] * state_jump
    first_lift = (lax.slice_in_dim(common, 0, elements, 1, axis_dim) - lax.slice_in_dim(flux_right, 0, elements, 1, axis_dim)) / EDGE_WEIGHT
    last_lift = (lax.slice_in_dim(flux_left, 1, elements + 1, 1, axis_dim) - lax.slice_in_dim(common, 1, elements + 1, 1, axis_dim)) / EDGE_WEIGHT
    zero_lift = jnp.zeros_like(first_lift)
    surface = jnp.stack([first_lift, zero_lift, zero_lift, zero_lift, last_lift], axis=axis_dim + 1).reshape(volume.shape)
    return surface - volume

def euler_parts(state, direction):
    density = state[0]
    velocity = state[1 + direction] / density
    kinetic = 0.5 * (state[1] * state[1] + state[2] * state[2] + state[3] * state[3]) / density
    pressure = (HEAT_RATIO - 1.0) * (state[4] - kinetic)
    return (density, velocity, pressure)

def euler_flux(state, direction):
    density, velocity, pressure = euler_parts(state, direction)
    pieces = [state[1 + direction]]
    for k in range(3):
        if k == direction:
            pieces.append(state[1 + k] * velocity + pressure)
        else:
            pieces.append(state[1 + k] * velocity)
    pieces.append((state[4] + pressure) * velocity)
    return jnp.stack(pieces)

def euler_speed(state, direction):
    density, velocity, pressure = euler_parts(state, direction)
    return jnp.abs(velocity) + jnp.sqrt(HEAT_RATIO * pressure / density)

def ape_flux(state, direction):
    pressure = state[0]
    carried = state[6] * state[1] + state[7] * state[2] + state[8] * state[3] + pressure / state[4]
    leading = state[5] * state[5] * state[4] * state[1 + direction] + state[6 + direction] * pressure
    pieces = [leading]
    for k in range(3):
        if k == direction:
            pieces.append(carried)
        else:
            pieces.append(jnp.zeros_like(carried))
    return jnp.stack(pieces)

def ape_speed(state, direction):
    return jnp.abs(state[6 + direction]) + state[5]

def extend(values, axis_dim):
    extent = values.shape[axis_dim]
    if axis_dim == 1:
        leading = lax.slice_in_dim(values, extent - 1, extent, 1, axis_dim)
        trailing = lax.slice_in_dim(values, 0, 1, 1, axis_dim)
    else:
        leading = lax.slice_in_dim(values, 0, 1, 1, axis_dim)
        trailing = lax.slice_in_dim(values, extent - 1, extent, 1, axis_dim)
    return jnp.concatenate([leading, values, trailing], axis=axis_dim)

def lamb_vector(state, derivative):
    density = state[0]
    velocity = [state[1 + k] / density for k in range(3)]
    omega_first = along_axis(velocity[2], derivative, 1) - along_axis(velocity[1], derivative, 2)
    omega_second = along_axis(velocity[0], derivative, 2) - along_axis(velocity[2], derivative, 0)
    omega_third = along_axis(velocity[1], derivative, 0) - along_axis(velocity[0], derivative, 1)
    return jnp.stack([omega_second * velocity[2] - omega_third * velocity[1], omega_third * velocity[0] - omega_first * velocity[2], omega_first * velocity[1] - omega_second * velocity[0]])

def take_rows(window_block, index_block):
    return jnp.take(window_block, index_block, axis=0)

def reference(les_state, acoustic_state, mean_density, mean_sound, mean_velocity, projection, intersection_counts, intersection_elem, intersection_pattern):
    derivative = gll_derivative()
    les_total = jnp.zeros_like(les_state)
    for direction in range(3):
        les_total = les_total + line_term(les_state, extend(les_state, direction + 1), partial(euler_flux, direction=direction), partial(euler_speed, direction=direction), 5, direction + 1, derivative)
    les_next = les_state + TIME_STEP * les_total
    blocks_count = N_AZIM * N_RAD * N_GROUP
    lamb = lamb_vector(les_state, derivative)
    lamb_blocks = lamb.reshape(3, N_AZIM, EA, 5, N_RAD, ER, 5, N_GROUP, EX, 5)
    rows = lamb_blocks.transpose(1, 4, 7, 2, 5, 8, 0, 3, 6, 9).reshape(N_AZIM, N_RAD, N_GROUP, EA * ER * EX, 375)
    column = jnp.roll(rows[:, :, :, :ER * EX], -1, axis=0)
    window = jnp.concatenate([rows, column], axis=3).reshape(blocks_count, EA * ER * EX + ER * EX, 375)
    elem_flat = intersection_elem.reshape(blocks_count, OVL)
    gathered = jax.vmap(take_rows)(window, elem_flat)
    running_ends = jnp.cumsum(intersection_counts.reshape(blocks_count, AEL), axis=1)
    positions = jnp.arange(OVL, dtype=jnp.int32)
    owner = lax.optimization_barrier(jnp.sum((positions[None, :, None] >= running_ends[:, None, :]).astype(jnp.int32), axis=2))
    block_ids = jnp.arange(blocks_count, dtype=jnp.int32)[:, None]
    segment = block_ids * (AEL * PAT) + owner * PAT + intersection_pattern.reshape(blocks_count, OVL)
    summed = jax.ops.segment_sum(gathered.reshape(blocks_count * OVL, 375), segment.reshape(-1), num_segments=blocks_count * AEL * PAT)
    summed = summed.reshape(blocks_count, AEL, PAT, 3, 125)
    projected = jnp.einsum('dapcn,pmn->dacm', summed, projection, precision=lax.Precision.HIGHEST)
    sources = projected.reshape(N_AZIM, N_RAD, N_GROUP, AA, AR, EX, 3, 5, 5, 5)
    sources = sources.transpose(6, 0, 3, 7, 1, 4, 8, 2, 5, 9).reshape(3, 5 * AA * N_AZIM, 5 * AR * N_RAD, 5 * EX * N_GROUP)
    combined = jnp.concatenate([acoustic_state, mean_density[None], mean_sound[None], mean_velocity], axis=0)
    ape_total = jnp.zeros_like(acoustic_state)
    for direction in range(3):
        ape_total = ape_total + line_term(combined, extend(combined, direction + 1), partial(ape_flux, direction=direction), partial(ape_speed, direction=direction), 4, direction + 1, derivative)
    forcing = jnp.concatenate([jnp.zeros_like(sources[:1]), sources], axis=0)
    acoustic_next = acoustic_state + TIME_STEP * (ape_total - forcing)
    return (les_next, acoustic_next)
```

```python
import functools
import math

import jax
import jax.numpy as jnp
import numpy as np
from jax import lax
from jax.experimental import pallas as pl
from jax.experimental.pallas import tpu as pltpu
from jax.sharding import PartitionSpec as P

GAMMA = 1.4
DT = 0.05
LIFT = 10.0
F32 = jnp.float32
BF16 = jnp.bfloat16
NX = 640
NE = 128
VMEM_LIMIT = 48 * 1024 * 1024


def derivative_matrix():
    points = np.array([-1.0, -math.sqrt(3.0 / 7.0), 0.0, math.sqrt(3.0 / 7.0), 1.0])
    weights = np.array([1.0 / np.prod([points[j] - points[k] for k in range(5) if k != j]) for j in range(5)])
    matrix = np.zeros((5, 5))
    for i in range(5):
        for j in range(5):
            if i != j:
                matrix[i, j] = weights[j] / weights[i] / (points[i] - points[j])
        matrix[i, i] = -np.sum(matrix[i])
    return matrix


D = derivative_matrix()
T = -D.copy()
T[0, 0] -= LIFT
T[4, 4] += LIFT


def lane_split():
    p = np.zeros((NX, NX), np.float32)
    for e in range(NE):
        for j in range(5):
            p[5 * e + j, NE * j + e] = 1.0
    return p


def radial_coefs():
    inner, outer = T.copy(), T.copy()
    inner[0, 0] += LIFT
    outer[4, 4] -= LIFT
    out = np.zeros((4, 5, 8, 128), np.float32)
    for kind, m in enumerate((inner, outer, D, -D)):
        for k in range(5):
            out[kind, k, :5, :] = m[:, k][:, None]
    return out


def apply5(f, m):
    s = [f[0] + f[4], f[1] + f[3]]
    d = [f[0] - f[4], f[1] - f[3]]
    out = [None] * 5
    for i in range(2):
        even = (0.5 * (m[i, 0] + m[i, 4])) * s[0] + (0.5 * (m[i, 1] + m[i, 3])) * s[1] + m[i, 2] * f[2]
        odd = (0.5 * (m[i, 0] - m[i, 4])) * d[0] + (0.5 * (m[i, 1] - m[i, 3])) * d[1]
        out[i] = odd + even
        out[4 - i] = odd - even
    out[2] = (0.5 * (m[2, 0] - m[2, 4])) * d[0] + (0.5 * (m[2, 1] - m[2, 3])) * d[1]
    return out


def radial(f, coefs):
    total = coefs[0] * f[0:1, :]
    for k in range(1, 5):
        total = total + coefs[k] * f[k : k + 1, :]
    return total


def tile(j):
    return slice(NE * j, NE * j + NE)


def wide(ref):
    return jnp.concatenate([ref[j] for j in range(ref.shape[0])], axis=1)


def split(x):
    hi = x.astype(BF16)
    return hi, (x - hi.astype(F32)).astype(BF16)


def dot(a, b):
    return jnp.dot(a, b, preferred_element_type=F32)


def relane(x, matrix):
    rows = x.shape[0]
    y = dot(jnp.concatenate(split(x), axis=0), matrix)
    return y[:rows] + y[rows:]


def les_prims(q):
    rec = 1.0 / q[0]
    v = [q[1] * rec, q[2] * rec, q[3] * rec]
    p = 0.4 * (q[4] - 0.5 * (q[1] * v[0] + q[2] * v[1] + q[3] * v[2]))
    return rec, v, p


def les_flux(q, v, p, k):
    out = [q[1 + k]]
    for j in range(3):
        out.append(q[1 + j] * v[k] + p if j == k else q[1 + j] * v[k])
    out.append((q[4] + p) * v[k])
    return out


def les_speed(rec, v, p, k):
    return jnp.abs(v[k]) + jnp.sqrt(GAMMA * p * rec)


def common(fl, fr, sl, sr, ql, qr):
    half = 0.5 * jnp.maximum(sl, sr)
    return [0.5 * (fl[n] + fr[n]) - half * (qr[n] - ql[n]) for n in range(len(fl))]


def ape_carried(s):
    return s[6] * s[1] + s[7] * s[2] + s[8] * s[3] + s[0] / s[4]


def ape_leading(s, k):
    return s[5] * s[5] * s[4] * s[1 + k] + s[6 + k] * s[0]


def ape_common(l, r, k, fl=None, fr=None):
    if fl is None:
        fl = (ape_leading(l, k), ape_carried(l))
    if fr is None:
        fr = (ape_leading(r, k), ape_carried(r))
    half = 0.5 * jnp.maximum(jnp.abs(l[6 + k]) + l[5], jnp.abs(r[6 + k]) + r[5])
    out = []
    for n in range(4):
        value = -half * (r[n] - l[n])
        if n == 0:
            value = value + 0.5 * (fl[0] + fr[0])
        elif n == 1 + k:
            value = value + 0.5 * (fl[1] + fr[1])
        out.append(value)
    return out, fl, fr


B_ROWS, F_ROWS, G_ROWS = 224, 96, 160
B_APE = 176
F_APE = 50


def pack_kernel(les, ac, den, snd, mv, back, fwd, low, high, axial):
    for a in range(5):
        rec = 1.0 / les[0, a]
        for c in range(3):
            v = les[1 + c, a] * rec
            for j in range(5):
                back[j, c * 50 + a * 10 : c * 50 + a * 10 + 10, :] = v[:, tile(j)]
    for j in range(5):
        back[j, 150:160, :] = les[0, 0, :, tile(j)]
        back[j, 160:170, :] = les[4, 0, :, tile(j)]
        back[j, 170:176, :] = jnp.zeros((6, 128), F32)
        back[j, 221:224, :] = jnp.zeros((3, 128), F32)
        for buf, a, base in ((back, 0, B_APE), (fwd, 4, F_APE)):
            for r in range(5):
                buf[j, pl.ds(base + r, 4, stride=5), :] = ac[a, r, :, tile(j)]
                buf[j, pl.ds(base + 30 + r, 3, stride=5), :] = mv[a, r, :, tile(j)]
            buf[j, base + 20 : base + 25, :] = den[a, :, tile(j)]
            buf[j, base + 25 : base + 30, :] = snd[a, :, tile(j)]
        for c in range(5):
            fwd[j, c * 10 : c * 10 + 10, :] = les[c, 9, :, tile(j)]
        for buf, r, ra in ((low, 0, 0), (high, 9, 4)):
            for c in range(5):
                for a in range(10):
                    buf[j, c * 10 + a : c * 10 + a + 1, :] = les[c, a, r : r + 1, tile(j)]
            for a in range(5):
                buf[j, pl.ds(F_APE + a, 4, stride=5), :] = ac[a, ra, :, tile(j)]
                buf[j, pl.ds(F_APE + 30 + a, 3, stride=5), :] = mv[a, ra, :, tile(j)]
                buf[j, F_APE + 20 + a : F_APE + 21 + a, :] = den[a, ra : ra + 1, tile(j)]
                buf[j, F_APE + 25 + a : F_APE + 26 + a, :] = snd[a, ra : ra + 1, tile(j)]
        for buf in (fwd, low, high):
            buf[j, 95:96, :] = jnp.zeros((1, 128), F32)
    first = lax.axis_index("group") == 0

    def end(ref, *at):
        return jnp.where(first, ref[(*at, slice(None), slice(NX - 1, NX))], ref[(*at, slice(None), slice(0, 1))])

    def gather(columns, rows):
        lane = lax.broadcasted_iota(jnp.int32, (rows, 128), 1)
        value = jnp.broadcast_to(columns[0], (rows, 128))
        for i in range(1, len(columns)):
            value = jnp.where(lane == i, jnp.broadcast_to(columns[i], (rows, 128)), value)
        return value

    for c in range(5):
        axial[16 * c : 16 * c + 10, :] = gather([end(les, c, a) for a in range(10)], 10)
        axial[16 * c + 10 : 16 * c + 16, :] = jnp.ones((6, 128), F32)
    axial[80:84, :] = gather([end(ac, a, r) for a in range(5) for r in range(5)], 4)
    axial[84:87, :] = gather([end(mv, a, r) for a in range(5) for r in range(5)], 3)
    axial[87:88, :] = jnp.zeros((1, 128), F32)
    axial[88:93, :] = gather([end(den, a) for a in range(5)], 5)
    axial[93:96, :] = jnp.zeros((3, 128), F32)
    axial[96:101, :] = gather([end(snd, a) for a in range(5)], 5)
    axial[101:160, :] = jnp.zeros((59, 128), F32)


def project(s, pp_hi, pp_lo, rhs_hi, rhs_lo, osc):
    for p in range(8):
        for c in range(3):
            hi, lo = split(s[c * 128 : c * 128 + 128, tile(p)])
            rhs_hi[p * 128 : p * 128 + 128, tile(c)] = hi
            rhs_lo[p * 128 : p * 128 + 128, tile(c)] = lo
    hi = rhs_hi[...]
    out = dot(pp_hi[...], hi) + (dot(pp_lo[...], hi) + dot(pp_hi[...], rhs_lo[...]))
    for c in range(3):
        osc[c] = out[:, tile(c)]


def interior_kernel(
    les, ac, den, snd, mv, proj, counts, elem, pattern, perm, perm_t, coef,
    les_out, ac_out, mn_out, pp_hi, pp_lo,
    y, acc, vel, omega, rt, m_own, one_hot, owned, s_own, rhs_hi, rhs_lo, osc, la, ya, da, flat,
):
    upper = lax.broadcasted_iota(jnp.int32, (NE, NE), 1)
    lower = lax.broadcasted_iota(jnp.int32, (NE, NE), 0)
    row = jnp.broadcast_to(counts[...], (NE, NE)).astype(F32)
    ends = jnp.sum(jnp.where(upper <= lower, row, 0.0), axis=1, keepdims=True)
    starts = jnp.sum(jnp.where(upper < lower, row, 0.0), axis=1, keepdims=True)
    position = lax.broadcasted_iota(jnp.int32, (NE, 768), 1).astype(F32)
    mine = jnp.where((position >= starts) & (position < ends), jnp.broadcast_to(pattern[...], (NE, 768)), -1)
    for p in range(8):
        owned[p * NE : p * NE + NE, :] = jnp.where(mine == p, 1.0, 0.0).astype(BF16)
    source = jnp.broadcast_to(elem[...], (NE, 768))
    for i in range(6):
        which = lax.broadcasted_iota(jnp.int32, (NE, 768), 0) + i * NE
        one_hot[i * NE : i * NE + NE, :] = jnp.where(which == source, 1.0, 0.0).astype(BF16)

    @pl.loop(0, 4)
    def _(i):
        rows = pl.ds(pl.multiple_of(i * NE, NE), NE)
        m_own[rows, :] = lax.dot_general(
            one_hot[rows, :], owned[...], (((1,), (1,)), ((), ())), preferred_element_type=F32
        ).astype(BF16)

    for i in range(2):
        mn_out[i * NE : i * NE + NE, :] = lax.dot_general(
            one_hot[(4 + i) * NE : (5 + i) * NE, :], owned[...], (((1,), (1,)), ((), ())), preferred_element_type=F32
        ).astype(BF16)

    flat[...] = jnp.zeros((1024, 128), F32)
    flat[0:1000, 0:125] = proj[...]
    for p in range(8):
        hi, lo = split(flat[pl.ds(p, 128, stride=8), :])
        pp_hi[:, tile(p)] = hi
        pp_lo[:, tile(p)] = lo

    @pl.loop(0, 5)
    def _(c):
        x0 = les[c, :, 0:8, :].reshape(80, NX)
        x1 = pltpu.roll(les[c, :, 2:10, :], 5, 1).reshape(80, NX)
        value = relane(jnp.concatenate([x0, x1], axis=0), perm[...])
        for j in range(5):
            y[c, j] = value[:, tile(j)]

    lane = lax.broadcasted_iota(jnp.int32, (8, 128), 1)

    @pl.loop(0, 20)
    def _(t):
        er = t // 10
        rows = pl.ds(pl.multiple_of(t * 8, 8), 8)
        q = [[y[c, j, rows, :] for j in range(5)] for c in range(5)]
        rec, v, p = [], [[], [], []], []
        for j in range(5):
            rec_j, v_j, p_j = les_prims([q[c][j] for c in range(5)])
            rec.append(rec_j)
            p.append(p_j)
            for k in range(3):
                v[k].append(v_j[k])
                vel[k, j, rows, :] = v_j[k]
            vel[3, j, rows, :] = p_j
        coefs = [coef[er, k] for k in range(5)]
        flux = [les_flux([q[c][j] for c in range(5)], [v[k][j] for k in range(3)], p[j], 2) for j in range(5)]
        s_left = les_speed(rec[4], [v[k][4] for k in range(3)], p[4], 2)
        s_right = pltpu.roll(les_speed(rec[0], [v[k][0] for k in range(3)], p[0], 2), 127, 1)
        half = 0.5 * jnp.maximum(s_left, s_right)
        for n in range(5):
            fr = pltpu.roll(flux[0][n], 127, 1)
            qr = pltpu.roll(q[n][0], 127, 1)
            h = 0.5 * (flux[4][n] + fr) - half * (qr - q[n][4])
            out = apply5([flux[j][n] for j in range(5)], T)
            out[4] = out[4] - LIFT * jnp.where(lane < 127, h, flux[4][n])
            out[0] = out[0] + LIFT * jnp.where(lane > 0, pltpu.roll(h, 1, 1), flux[0][n])
            for j in range(5):
                f = les_flux([q[c][j] for c in range(5)], [v[k][j] for k in range(3)], p[j], 1)[n]
                acc[n, j, rows, :] = out[j] + radial(f, coefs)
        dcoefs = [coef[2, k] for k in range(5)]
        d2v0 = apply5(v[0], D)
        d2v1 = apply5(v[1], D)
        for j in range(5):
            omega[0, j, rows, :] = radial(v[2][j], dcoefs) - d2v1[j]
            omega[1, j, rows, :] = d2v0[j]
            omega[2, j, rows, :] = -radial(v[0][j], dcoefs)

    for c in range(3):
        for i in range(4):
            rt[i, c * 128 + 120 : c * 128 + 128, :] = jnp.zeros((8, 128), F32)

    @pl.loop(0, 2)
    def _(er):
        for j in range(5):
            at = [pl.ds(pl.multiple_of(er * 80 + a * 8, 8), 8) for a in range(10)]
            q = [[y[c, j, at[a], :] for a in range(10)] for c in range(5)]
            v = [[vel[k, j, at[a], :] for a in range(10)] for k in range(3)]
            p = [vel[3, j, at[a], :] for a in range(10)]
            flux = [les_flux([q[c][a] for c in range(5)], [v[k][a] for k in range(3)], p[a], 0) for a in range(10)]
            speed = [
                jnp.abs(v[0][a]) + jnp.sqrt(GAMMA * p[a] / q[0][a]) for a in (4, 5)
            ]
            h = common(flux[4], flux[5], speed[0], speed[1], [q[c][4] for c in range(5)], [q[c][5] for c in range(5)])
            for n in range(5):
                low = apply5([flux[a][n] for a in range(5)], T)
                low[0] = low[0] + LIFT * flux[0][n]
                low[4] = low[4] - LIFT * h[n]
                top = apply5([flux[5 + a][n] for a in range(5)], T)
                top[0] = top[0] + LIFT * h[n]
                top[4] = top[4] - LIFT * flux[9][n]
                for a, value in enumerate(low + top):
                    acc[n, j, at[a], :] = acc[n, j, at[a], :] + value
            for ea in range(2):
                d0v1 = apply5([v[1][5 * ea + i] for i in range(5)], D)
                d0v2 = apply5([v[2][5 * ea + i] for i in range(5)], D)
                for i in range(5):
                    a = 5 * ea + i
                    w0 = omega[0, j, at[a], :]
                    w1 = omega[1, j, at[a], :] - d0v2[i]
                    w2 = omega[2, j, at[a], :] + d0v1[i]
                    lamb = [
                        w1 * v[2][a] - w2 * v[1][a],
                        w2 * v[0][a] - w0 * v[2][a],
                        w0 * v[1][a] - w1 * v[0][a],
                    ]
                    for c in range(3):
                        rt[2 * ea + er, pl.ds(c * 128 + i * 25 + j, 5, stride=5), :] = lamb[c][0:5]

    for j in range(5):
        left, right = pl.ds(4, 10, stride=8), pl.ds(80, 10, stride=8)
        ql = [y[c, j, left, :] for c in range(5)]
        qr = [y[c, j, right, :] for c in range(5)]
        rl, vl, pl_ = les_prims(ql)
        rr, vr, pr = les_prims(qr)
        h = common(
            les_flux(ql, vl, pl_, 1), les_flux(qr, vr, pr, 1),
            les_speed(rl, vl, pl_, 1), les_speed(rr, vr, pr, 1), ql, qr,
        )
        for n in range(5):
            acc[n, j, left, :] = acc[n, j, left, :] - LIFT * h[n]
            acc[n, j, right, :] = acc[n, j, right, :] + LIFT * h[n]

    @pl.loop(0, 5)
    def _(c):
        delta = relane(jnp.concatenate([acc[c, j] for j in range(5)], axis=1), perm_t[...]).reshape(2, 10, 8, NX)
        les_out[c, :, 0:5, :] = les[c, :, 0:5, :] + DT * delta[0, :, 0:5, :]
        les_out[c, :, 5:10, :] = les[c, :, 5:10, :] + DT * delta[1, :, 0:5, :]

    hi, lo = split(wide(rt))
    m = m_own[...]
    s_own[...] = dot(hi, m) + dot(lo, m)
    project(s_own, pp_hi, pp_lo, rhs_hi, rhs_lo, osc)

    for a in range(5):
        for r in range(5):
            la[a * 20 + r * 4 : a * 20 + r * 4 + 4, :] = ac[a, r]
            la[104 + a * 15 + r * 3 : 104 + a * 15 + r * 3 + 3, :] = mv[a, r]
        la[184 + a * 8 : 184 + a * 8 + 5, :] = den[a]
        la[224 + a * 8 : 224 + a * 8 + 5, :] = snd[a]
    value = relane(la[...], perm[...])
    for j in range(5):
        ya[j] = value[:, tile(j)]
    lane5 = lax.broadcasted_iota(jnp.int32, (5, 128), 1)
    state = [[None] * 5 for _ in range(5)]
    for a in range(5):
        for j in range(5):
            state[a][j] = (
                [ya[j, pl.ds(a * 20 + c, 5, stride=4), :] for c in range(4)]
                + [ya[j, 184 + a * 8 : 189 + a * 8, :], ya[j, 224 + a * 8 : 229 + a * 8, :]]
                + [ya[j, pl.ds(104 + a * 15 + k, 5, stride=3), :] for k in range(3)]
            )
    carried = [[ape_carried(state[a][j]) for j in range(5)] for a in range(5)]
    lead = [[[ape_leading(state[a][j], k) for j in range(5)] for a in range(5)] for k in range(3)]
    total = [[[None] * 5 for _ in range(5)] for _ in range(4)]
    minus = -D
    mcoefs = [coef[3, k, 0:5] for k in range(5)]
    for j in range(5):
        first = apply5([lead[0][a][j] for a in range(5)], minus)
        other = apply5([carried[a][j] for a in range(5)], minus)
        for a in range(5):
            total[0][a][j] = first[a] + radial(lead[1][a][j], mcoefs)
            total[1][a][j] = other[a]
            total[2][a][j] = radial(carried[a][j], mcoefs)
    for a in range(5):
        first = apply5(lead[2][a], T)
        other = apply5(carried[a], T)
        shift = [pltpu.roll(jnp.pad(x, ((0, 3), (0, 0))), 127, 1)[0:5] for x in state[a][0]]
        h, fl, fr = ape_common(state[a][4], shift, 2)
        for n in range(4):
            own4 = lead[2][a][4] if n == 0 else carried[a][4] if n == 3 else jnp.zeros_like(carried[a][4])
            own0 = lead[2][a][0] if n == 0 else carried[a][0] if n == 3 else jnp.zeros_like(carried[a][0])
            back = pltpu.roll(jnp.pad(h[n], ((0, 3), (0, 0))), 1, 1)[0:5]
            lift4 = -LIFT * jnp.where(lane5 < 127, h[n], own4)
            lift0 = LIFT * jnp.where(lane5 > 0, back, own0)
            for j in range(5):
                value = total[n][a][j]
                if n in (0, 3):
                    extra = first[j] if n == 0 else other[j]
                    value = extra if value is None else value + extra
                if j == 4:
                    value = value + lift4
                if j == 0:
                    value = value + lift0
                if n > 0:
                    value = value - osc[n - 1, pl.ds(a * 25 + j, 5, stride=5), :]
                da[j, pl.ds(a * 20 + n, 5, stride=4), :] = value
    for j in range(5):
        da[j, 100:104, :] = jnp.zeros((4, 128), F32)
    delta = relane(wide(da), perm_t[...])
    for a in range(5):
        for r in range(5):
            i = (a * 5 + r) * 4
            ac_out[a, r] = ac[a, r] + DT * delta[i : i + 4]


def ape_face(buf, base, j):
    return [buf[j, base + 5 * n : base + 5 * n + 5, :] for n in range(9)]


def back_face(buf, j):
    rho = buf[j, 150:160, :]
    return [rho] + [rho * buf[j, c * 50 : c * 50 + 10, :] for c in range(3)] + [buf[j, 160:170, :]]


def les_rows(buf, j):
    return [buf[j, c * 10 : c * 10 + 10, :] for c in range(5)]


def les_common(ql, qr, k):
    rl, vl, pl_ = les_prims(ql)
    rr, vr, pr = les_prims(qr)
    fl, fr = les_flux(ql, vl, pl_, k), les_flux(qr, vr, pr, k)
    return common(fl, fr, les_speed(rl, vl, pl_, k), les_speed(rr, vr, pr, k), ql, qr), fl, fr


def faces_kernel(
    les_in, ac_in, back, fwd, low, high, axial, fwd_in, low_in, high_in, axial_in, les_out, ac_out, sub, azim, aub,
):
    rad = lax.axis_index("rad")
    first_half = lax.axis_index("group") == 0
    at_low, at_high = rad == 0, rad == lax.axis_size("rad") - 1
    for j in range(5):
        own_low, own_high = les_rows(low, j), les_rows(high, j)
        nbr_low = [jnp.where(at_low, o, n) for o, n in zip(own_low, les_rows(low_in, j))]
        nbr_high = [jnp.where(at_high, o, n) for o, n in zip(own_high, les_rows(high_in, j))]
        h, _, fr = les_common(nbr_low, own_low, 1)
        g, fl, _ = les_common(own_high, nbr_high, 1)
        for n in range(5):
            sub[n * 24 : n * 24 + 10, tile(j)] = DT * LIFT * (h[n] - fr[n])
            sub[n * 24 + 10 : n * 24 + 20, tile(j)] = DT * LIFT * (fl[n] - g[n])
        h, _, fr = les_common(les_rows(fwd_in, j), back_face(back, j), 0)
        for n in range(5):
            azim[n * 16 : n * 16 + 10, tile(j)] = DT * LIFT * (h[n] - fr[n])
    own = [axial[16 * c : 16 * c + 16, :] for c in range(5)]
    nbr = [axial_in[16 * c : 16 * c + 16, :] for c in range(5)]
    ql = [jnp.where(first_half, o, n) for o, n in zip(own, nbr)]
    qr = [jnp.where(first_half, n, o) for o, n in zip(own, nbr)]
    h, fl, fr = les_common(ql, qr, 2)
    axis = [DT * LIFT * jnp.where(first_half, fl[n] - h[n], h[n] - fr[n]) for n in range(5)]
    lane = lax.broadcasted_iota(jnp.int32, (10, 128), 1)
    on_last = (lane == 127) & first_half
    on_first = (lane == 0) & jnp.logical_not(first_half)
    for n in range(5):
        for a in range(10):
            value = les_in[n, a]
            column = jnp.broadcast_to(axis[n][0:10, a : a + 1], (10, 128))
            head = value[:, 0:128] + jnp.where(on_first, column, 0.0)
            tail = value[:, 512:640] + jnp.where(on_last, column, 0.0)
            value = jnp.concatenate([head, value[:, 128:512], tail], axis=1)
            if a == 0:
                value = value + azim[n * 16 : n * 16 + 10, :]
            les_out[n, a] = value
            les_out[n, a, 0:1, :] = les_out[n, a, 0:1, :] + sub[n * 24 + a : n * 24 + a + 1, :]
            les_out[n, a, 9:10, :] = les_out[n, a, 9:10, :] + sub[n * 24 + 10 + a : n * 24 + 11 + a, :]

    for j in range(5):
        aub[j] = jnp.zeros((104, 128), F32)
        h, _, fr = ape_common(ape_face(fwd_in, F_APE, j), ape_face(back, B_APE, j), 0)
        for n in range(4):
            own_flux = fr[0] if n == 0 else fr[1] if n == 1 else 0.0
            aub[j, pl.ds(n, 5, stride=4), :] = DT * LIFT * (h[n] - own_flux)
        own_l, own_h = ape_face(low, F_APE, j), ape_face(high, F_APE, j)
        nbr_l = [jnp.where(at_low, o, n) for o, n in zip(own_l, ape_face(low_in, F_APE, j))]
        nbr_h = [jnp.where(at_high, o, n) for o, n in zip(own_h, ape_face(high_in, F_APE, j))]
        h, _, fr = ape_common(nbr_l, own_l, 1)
        g, fl, _ = ape_common(own_h, nbr_h, 1)
        for n in range(4):
            fr_n = fr[0] if n == 0 else fr[1] if n == 2 else 0.0
            fl_n = fl[0] if n == 0 else fl[1] if n == 2 else 0.0
            at = pl.ds(n, 5, stride=20)
            aub[j, at, :] = aub[j, at, :] + DT * LIFT * (h[n] - fr_n)
            at = pl.ds(16 + n, 5, stride=20)
            aub[j, at, :] = aub[j, at, :] + DT * LIFT * (fl_n - g[n])

    def axial_state(buf):
        def spread(base):
            rows = buf[base : base + 8, :]
            row = lax.broadcasted_iota(jnp.int32, (8, 128), 0)
            lanes = lax.broadcasted_iota(jnp.int32, (8, 128), 1)
            wide = jnp.zeros((8, 128), F32)
            for a in range(5):
                wide = jnp.where((lanes == a * 5 + row) & (row < 5), jnp.broadcast_to(rows[:, a : a + 1], (8, 128)), wide)
            return jnp.sum(wide, axis=0, keepdims=True)

        ones = lax.broadcasted_iota(jnp.int32, (1, 128), 1) < 25
        return (
            [buf[80 + c : 81 + c, :] for c in range(4)]
            + [jnp.where(ones, spread(88), 1.0), spread(96)]
            + [buf[84 + k : 85 + k, :] for k in range(3)]
        )

    own, nbr = axial_state(axial), axial_state(axial_in)
    ql = [jnp.where(first_half, o, n) for o, n in zip(own, nbr)]
    qr = [jnp.where(first_half, n, o) for o, n in zip(own, nbr)]
    h, fl, fr = ape_common(ql, qr, 2)
    rows = []
    for n in range(4):
        fl_n = fl[0] if n == 0 else fl[1] if n == 3 else 0.0
        fr_n = fr[0] if n == 0 else fr[1] if n == 3 else 0.0
        rows.append(DT * LIFT * jnp.where(first_half, fl_n - h[n], h[n] - fr_n))
    axis = jnp.concatenate(rows, axis=0)
    lane4 = lax.broadcasted_iota(jnp.int32, (4, 128), 1)
    on_last = (lane4 == 127) & first_half
    on_first = (lane4 == 0) & jnp.logical_not(first_half)
    for a in range(5):
        for r in range(5):
            i = a * 5 + r
            value = ac_in[a, r] + jnp.concatenate([aub[j, 4 * i : 4 * i + 4, :] for j in range(5)], axis=1)
            column = jnp.broadcast_to(axis[:, i : i + 1], (4, 128))
            head = value[:, 0:128] + jnp.where(on_first, column, 0.0)
            tail = value[:, 512:640] + jnp.where(on_last, column, 0.0)
            ac_out[a, r] = jnp.concatenate([head, value[:, 128:512], tail], axis=1)


def finish_kernel(
    les_in, ac_in, back_in, fwd, mn, pp_hi, pp_lo, perm, perm_t, coef,
    les_out, ac_out, yn, rt, s_nbr, rhs_hi, rhs_lo, osc, da,
):
    yn[...] = relane(jnp.concatenate([back_in[j, 0:160, :] for j in range(5)], axis=1), perm[...])
    for c in range(3):
        for i in range(2):
            rt[i, c * 128 + 120 : c * 128 + 128, :] = jnp.zeros((8, 128), F32)
    dcoefs = [coef[2, k] for k in range(5)]
    for er in range(2):
        v = [
            [[yn[c * 50 + a * 10 + er * 5 : c * 50 + a * 10 + er * 5 + 8, tile(j)] for j in range(5)] for a in range(5)]
            for c in range(3)
        ]
        d2v0 = [apply5(v[0][a], D) for a in range(5)]
        d2v1 = [apply5(v[1][a], D) for a in range(5)]
        for j in range(5):
            d0v1 = apply5([v[1][a][j] for a in range(5)], D)
            d0v2 = apply5([v[2][a][j] for a in range(5)], D)
            for a in range(5):
                w0 = radial(v[2][a][j], dcoefs) - d2v1[a][j]
                w1 = d2v0[a][j] - d0v2[a]
                w2 = d0v1[a] - radial(v[0][a][j], dcoefs)
                lamb = [
                    w1 * v[2][a][j] - w2 * v[1][a][j],
                    w2 * v[0][a][j] - w0 * v[2][a][j],
                    w0 * v[1][a][j] - w1 * v[0][a][j],
                ]
                for c in range(3):
                    rt[er, pl.ds(c * 128 + a * 25 + j, 5, stride=5), :] = lamb[c][0:5]
    hi, lo = split(wide(rt))
    m = mn[...]
    s_nbr[...] = dot(hi, m) + dot(lo, m)
    project(s_nbr, pp_hi, pp_lo, rhs_hi, rhs_lo, osc)
    for j in range(5):
        da[j] = jnp.zeros((104, 128), F32)
        for a in range(5):
            for n in range(1, 4):
                da[j, pl.ds(a * 20 + n, 5, stride=4), :] = osc[n - 1, pl.ds(a * 25 + j, 5, stride=5), :]
    delta = relane(wide(da), perm_t[...])
    for j in range(5):
        h, fl, _ = les_common(les_rows(fwd, j), back_face(back_in, j), 0)
        for n in range(5):
            les_out[n, 0, :, tile(j)] = les_in[n, 0, :, tile(j)] + DT * LIFT * (fl[n] - h[n])
        da[j] = delta[:, tile(j)]
        h, fl, _ = ape_common(ape_face(fwd, F_APE, j), ape_face(back_in, B_APE, j), 0)
        for n in range(4):
            own_flux = fl[0] if n == 0 else fl[1] if n == 1 else 0.0
            at = pl.ds(80 + n, 5, stride=4)
            da[j, at, :] = da[j, at, :] - LIFT * (own_flux - h[n])
        for a in range(5):
            for r in range(5):
                i = (a * 5 + r) * 4
                ac_out[a, r, :, tile(j)] = ac_in[a, r, :, tile(j)] - DT * da[j, i : i + 4, :]


def shape(*dims, dtype=F32):
    return jax.ShapeDtypeStruct(dims, dtype)


def cost(flops, size):
    return pl.CostEstimate(flops=flops, bytes_accessed=size, transcendentals=0)


def params():
    return pltpu.CompilerParams(vmem_limit_bytes=VMEM_LIMIT)


def body(les, ac, den, snd, mv, proj, counts, elem, pattern):
    vmem = pl.BlockSpec(memory_space=pltpu.VMEM)
    ac = jnp.transpose(ac, (1, 2, 0, 3))
    mv = jnp.transpose(mv, (1, 2, 0, 3))
    proj = jnp.transpose(proj, (1, 0, 2)).reshape(1000, 125)
    counts, elem, pattern = counts.reshape(1, 128), elem.reshape(1, 768), pattern.reshape(1, 768)
    perm = jnp.asarray(lane_split(), BF16)
    perm_t = jnp.asarray(lane_split().T, BF16)
    coef = jnp.asarray(radial_coefs(), F32)

    back, fwd, low, high, axial = pl.pallas_call(
        pack_kernel,
        out_shape=[shape(5, B_ROWS, 128)] + [shape(5, F_ROWS, 128)] * 3 + [shape(G_ROWS, 128)],
        in_specs=[vmem] * 5,
        out_specs=[vmem] * 5,
        compiler_params=params(),
        cost_estimate=cost(1_000_000, 5_000_000),
        name="pack",
    )(les, ac, den, snd, mv)

    azim, radc = lax.axis_size("azim"), lax.axis_size("rad")
    back_in = lax.ppermute(back, "azim", [(i, (i - 1) % azim) for i in range(azim)])
    fwd_in = lax.ppermute(fwd, "azim", [(i, (i + 1) % azim) for i in range(azim)])
    high_in = lax.ppermute(low, "rad", [(i, i - 1) for i in range(1, radc)])
    low_in = lax.ppermute(high, "rad", [(i, i + 1) for i in range(radc - 1)])
    axial_in = lax.ppermute(axial, "group", [(0, 1), (1, 0)])

    les_part, ac_part, mn, pp_hi, pp_lo = pl.pallas_call(
        interior_kernel,
        out_shape=[
            shape(5, 10, 10, NX), shape(5, 5, 4, NX), shape(256, 1024, dtype=BF16),
            shape(128, 1024, dtype=BF16), shape(128, 1024, dtype=BF16),
        ],
        in_specs=[vmem] * 12,
        out_specs=[vmem] * 5,
        scratch_shapes=[
            pltpu.VMEM((5, 5, 160, 128), F32),
            pltpu.VMEM((5, 5, 160, 128), F32),
            pltpu.VMEM((4, 5, 160, 128), F32),
            pltpu.VMEM((3, 5, 160, 128), F32),
            pltpu.VMEM((4, 384, 128), F32),
            pltpu.VMEM((512, 1024), BF16),
            pltpu.VMEM((768, 768), BF16),
            pltpu.VMEM((1024, 768), BF16),
            pltpu.VMEM((384, 1024), F32),
            pltpu.VMEM((1024, 384), BF16),
            pltpu.VMEM((1024, 384), BF16),
            pltpu.VMEM((3, 128, 128), F32),
            pltpu.VMEM((264, NX), F32),
            pltpu.VMEM((5, 264, 128), F32),
            pltpu.VMEM((5, 104, 128), F32),
            pltpu.VMEM((1024, 128), F32),
        ],
        compiler_params=params(),
        cost_estimate=cost(5_000_000_000, 10_000_000),
        name="interior",
    )(les, ac, den, snd, mv, proj, counts, elem, pattern, perm, perm_t, coef)

    les_part, ac_part = pl.pallas_call(
        faces_kernel,
        out_shape=[shape(5, 10, 10, NX), shape(5, 5, 4, NX)],
        in_specs=[vmem] * 11,
        out_specs=[vmem] * 2,
        scratch_shapes=[pltpu.VMEM((120, NX), F32), pltpu.VMEM((80, NX), F32), pltpu.VMEM((5, 104, 128), F32)],
        input_output_aliases={0: 0, 1: 1},
        compiler_params=params(),
        cost_estimate=cost(1_000_000, 5_000_000),
        name="faces",
    )(les_part, ac_part, back, fwd, low, high, axial, fwd_in, low_in, high_in, axial_in)

    plane = pl.BlockSpec((5, 1, 10, NX), lambda i: (0, 9, 0, 0))

    def whole(*dims):
        return pl.BlockSpec(dims, lambda i: (0,) * len(dims))

    les_next, ac_next = pl.pallas_call(
        finish_kernel,
        grid=(1,),
        out_shape=[shape(5, 10, 10, NX), shape(5, 5, 4, NX)],
        in_specs=[
            plane, whole(5, 5, 4, NX), whole(5, B_ROWS, 128), whole(5, F_ROWS, 128), whole(256, 1024), whole(128, 1024),
            whole(128, 1024), whole(NX, NX), whole(NX, NX), whole(4, 5, 8, 128),
        ],
        out_specs=[plane, whole(5, 5, 4, NX)],
        scratch_shapes=[
            pltpu.VMEM((160, NX), F32),
            pltpu.VMEM((2, 384, 128), F32),
            pltpu.VMEM((384, 1024), F32),
            pltpu.VMEM((1024, 384), BF16),
            pltpu.VMEM((1024, 384), BF16),
            pltpu.VMEM((3, 128, 128), F32),
            pltpu.VMEM((5, 104, 128), F32),
        ],
        input_output_aliases={0: 0, 1: 1},
        compiler_params=params(),
        cost_estimate=cost(500_000_000, 4_000_000),
        name="finish",
    )(les_part, ac_part, back_in, fwd, mn, pp_hi, pp_lo, perm, perm_t, coef)
    return les_next, jnp.transpose(ac_next, (2, 0, 1, 3))


def solution(mesh):
    field = P(None, "azim", "rad", "group")
    node = P("azim", "rad", "group")
    lists = P("azim", "rad", "group", None)
    return jax.shard_map(
        body,
        mesh=mesh,
        in_specs=(field, field, node, node, field, P(), lists, lists, lists),
        out_specs=(field, field),
        check_vma=False,
    )
```

```python
import functools
import math

import jax
import jax.numpy as jnp
import numpy as np
from jax import lax
from jax.experimental import pallas as pl
from jax.experimental.pallas import tpu as pltpu
from jax.sharding import PartitionSpec as P

GAMMA = 1.4
DT = 0.05
LIFT = 10.0
F32 = jnp.float32
BF16 = jnp.bfloat16
NX = 640
NE = 128
VMEM_LIMIT = 40 * 1024 * 1024


def derivative_matrix():
    points = np.array([-1.0, -math.sqrt(3.0 / 7.0), 0.0, math.sqrt(3.0 / 7.0), 1.0])
    weights = np.array([1.0 / np.prod([points[j] - points[k] for k in range(5) if k != j]) for j in range(5)])
    matrix = np.zeros((5, 5))
    for i in range(5):
        for j in range(5):
            if i != j:
                matrix[i, j] = weights[j] / weights[i] / (points[i] - points[j])
        matrix[i, i] = -np.sum(matrix[i])
    return matrix


D = derivative_matrix()
T = -D.copy()
T[0, 0] -= LIFT
T[4, 4] += LIFT


def lane_split():
    p = np.zeros((NX, NX), np.float32)
    for e in range(NE):
        for j in range(5):
            p[5 * e + j, NE * j + e] = 1.0
    return p


def radial_coefs():
    inner, outer = T.copy(), T.copy()
    inner[0, 0] += LIFT
    outer[4, 4] -= LIFT
    out = np.zeros((4, 5, 8, 128), np.float32)
    for kind, m in enumerate((inner, outer, D, -D)):
        for k in range(5):
            out[kind, k, :5, :] = m[:, k][:, None]
    return out


def apply5(f, m):
    s = [f[0] + f[4], f[1] + f[3]]
    d = [f[0] - f[4], f[1] - f[3]]
    out = [None] * 5
    for i in range(2):
        even = (0.5 * (m[i, 0] + m[i, 4])) * s[0] + (0.5 * (m[i, 1] + m[i, 3])) * s[1] + m[i, 2] * f[2]
        odd = (0.5 * (m[i, 0] - m[i, 4])) * d[0] + (0.5 * (m[i, 1] - m[i, 3])) * d[1]
        out[i] = odd + even
        out[4 - i] = odd - even
    out[2] = (0.5 * (m[2, 0] - m[2, 4])) * d[0] + (0.5 * (m[2, 1] - m[2, 3])) * d[1]
    return out


def radial(f, coefs):
    total = coefs[0] * f[0:1, :]
    for k in range(1, 5):
        total = total + coefs[k] * f[k : k + 1, :]
    return total


def tile(j):
    return slice(NE * j, NE * j + NE)


def wide(ref):
    return jnp.concatenate([ref[j] for j in range(ref.shape[0])], axis=1)


def split(x):
    hi = x.astype(BF16)
    return hi, (x - hi.astype(F32)).astype(BF16)


def dot(a, b):
    return jnp.dot(a, b, preferred_element_type=F32)


def relane(x, matrix):
    rows = x.shape[0]
    y = dot(jnp.concatenate(split(x), axis=0), matrix)
    return y[:rows] + y[rows:]


def les_prims(q):
    rec = 1.0 / q[0]
    v = [q[1] * rec, q[2] * rec, q[3] * rec]
    p = 0.4 * (q[4] - 0.5 * (q[1] * v[0] + q[2] * v[1] + q[3] * v[2]))
    return rec, v, p


def les_flux(q, v, p, k):
    out = [q[1 + k]]
    for j in range(3):
        out.append(q[1 + j] * v[k] + p if j == k else q[1 + j] * v[k])
    out.append((q[4] + p) * v[k])
    return out


def les_speed(rec, v, p, k):
    return jnp.abs(v[k]) + jnp.sqrt(GAMMA * p * rec)


def common(fl, fr, sl, sr, ql, qr):
    half = 0.5 * jnp.maximum(sl, sr)
    return [0.5 * (fl[n] + fr[n]) - half * (qr[n] - ql[n]) for n in range(len(fl))]


def ape_carried(s):
    return s[6] * s[1] + s[7] * s[2] + s[8] * s[3] + s[0] / s[4]


def ape_leading(s, k):
    return s[5] * s[5] * s[4] * s[1 + k] + s[6 + k] * s[0]


def ape_common(l, r, k, fl=None, fr=None):
    if fl is None:
        fl = (ape_leading(l, k), ape_carried(l))
    if fr is None:
        fr = (ape_leading(r, k), ape_carried(r))
    half = 0.5 * jnp.maximum(jnp.abs(l[6 + k]) + l[5], jnp.abs(r[6 + k]) + r[5])
    out = []
    for n in range(4):
        value = -half * (r[n] - l[n])
        if n == 0:
            value = value + 0.5 * (fl[0] + fr[0])
        elif n == 1 + k:
            value = value + 0.5 * (fl[1] + fr[1])
        out.append(value)
    return out, fl, fr


B_ROWS, F_ROWS, G_ROWS = 224, 96, 160
B_APE = 176
F_APE = 50


def pack_kernel(
    les_h, ac_h, den_h, snd_h, mv_h, back, fwd, low, high, axial, les, ac, den, snd, mv, sems,
):
    copies = [pltpu.make_async_copy(les_h.at[c], les.at[c], sems.at[c]) for c in range(5)]
    for i, (src, dst) in enumerate(((ac_h, ac), (den_h, den), (snd_h, snd), (mv_h, mv))):
        copies.append(pltpu.make_async_copy(src, dst, sems.at[5 + i]))
    for copy in copies:
        copy.start()
    for copy in copies:
        copy.wait()
    for a in range(5):
        rec = 1.0 / les[0, a]
        for c in range(3):
            v = les[1 + c, a] * rec
            for j in range(5):
                back[j, c * 50 + a * 10 : c * 50 + a * 10 + 10, :] = v[:, tile(j)]
    for j in range(5):
        back[j, 150:160, :] = les[0, 0, :, tile(j)]
        back[j, 160:170, :] = les[4, 0, :, tile(j)]
        back[j, 170:176, :] = jnp.zeros((6, 128), F32)
        back[j, 221:224, :] = jnp.zeros((3, 128), F32)
        for buf, a, base in ((back, 0, B_APE), (fwd, 4, F_APE)):
            for r in range(5):
                buf[j, pl.ds(base + r, 4, stride=5), :] = ac[a, r, :, tile(j)]
                buf[j, pl.ds(base + 30 + r, 3, stride=5), :] = mv[a, r, :, tile(j)]
            buf[j, base + 20 : base + 25, :] = den[a, :, tile(j)]
            buf[j, base + 25 : base + 30, :] = snd[a, :, tile(j)]
        for c in range(5):
            fwd[j, c * 10 : c * 10 + 10, :] = les[c, 9, :, tile(j)]
        for buf, r, ra in ((low, 0, 0), (high, 9, 4)):
            for c in range(5):
                for a in range(10):
                    buf[j, c * 10 + a : c * 10 + a + 1, :] = les[c, a, r : r + 1, tile(j)]
            for a in range(5):
                buf[j, pl.ds(F_APE + a, 4, stride=5), :] = ac[a, ra, :, tile(j)]
                buf[j, pl.ds(F_APE + 30 + a, 3, stride=5), :] = mv[a, ra, :, tile(j)]
                buf[j, F_APE + 20 + a : F_APE + 21 + a, :] = den[a, ra : ra + 1, tile(j)]
                buf[j, F_APE + 25 + a : F_APE + 26 + a, :] = snd[a, ra : ra + 1, tile(j)]
        for buf in (fwd, low, high):
            buf[j, 95:96, :] = jnp.zeros((1, 128), F32)
    first = lax.axis_index("group") == 0

    def end(ref, *at):
        return jnp.where(first, ref[(*at, slice(None), slice(NX - 1, NX))], ref[(*at, slice(None), slice(0, 1))])

    def gather(columns, rows):
        lane = lax.broadcasted_iota(jnp.int32, (rows, 128), 1)
        value = jnp.broadcast_to(columns[0], (rows, 128))
        for i in range(1, len(columns)):
            value = jnp.where(lane == i, jnp.broadcast_to(columns[i], (rows, 128)), value)
        return value

    for c in range(5):
        axial[16 * c : 16 * c + 10, :] = gather([end(les, c, a) for a in range(10)], 10)
        axial[16 * c + 10 : 16 * c + 16, :] = jnp.ones((6, 128), F32)
    axial[80:84, :] = gather([end(ac, a, r) for a in range(5) for r in range(5)], 4)
    axial[84:87, :] = gather([end(mv, a, r) for a in range(5) for r in range(5)], 3)
    axial[87:88, :] = jnp.zeros((1, 128), F32)
    axial[88:93, :] = gather([end(den, a) for a in range(5)], 5)
    axial[93:96, :] = jnp.zeros((3, 128), F32)
    axial[96:101, :] = gather([end(snd, a) for a in range(5)], 5)
    axial[101:160, :] = jnp.zeros((59, 128), F32)


ROWS = 768
APE, APE_MV, APE_DEN, APE_SND = 504, 608, 688, 728


def interior_kernel(
    les, ac, den, snd, mv, proj, counts, elem, pattern, perm, coef,
    acc, da, lamb_out, m_out, pp_hi, pp_lo,
    x, y, vel, omega, rt, one_hot, owned, flat,
):
    def list_matrices():
        upper = lax.broadcasted_iota(jnp.int32, (NE, NE), 1)
        lower = lax.broadcasted_iota(jnp.int32, (NE, NE), 0)
        row = jnp.broadcast_to(counts[...], (NE, NE)).astype(F32)
        ends = jnp.sum(jnp.where(upper <= lower, row, 0.0), axis=1, keepdims=True)
        starts = jnp.sum(jnp.where(upper < lower, row, 0.0), axis=1, keepdims=True)
        position = lax.broadcasted_iota(jnp.int32, (NE, 768), 1).astype(F32)
        mine = jnp.where((position >= starts) & (position < ends), jnp.broadcast_to(pattern[...], (NE, 768)), -1)
        for p in range(8):
            owned[p * NE : p * NE + NE, :] = jnp.where(mine == p, 1.0, 0.0).astype(BF16)
        source = jnp.broadcast_to(elem[...], (NE, 768))
        for i in range(6):
            which = lax.broadcasted_iota(jnp.int32, (NE, 768), 0) + i * NE
            one_hot[i * NE : i * NE + NE, :] = jnp.where(which == source, 1.0, 0.0).astype(BF16)
        m_out[...] = lax.dot_general(
            one_hot[...], owned[...], (((1,), (1,)), ((), ())), preferred_element_type=F32
        ).astype(BF16)

    def projection_matrices():
        flat[...] = jnp.zeros((1024, 128), F32)
        flat[0:1000, 0:125] = proj[...]
        for p in range(8):
            hi, lo = split(flat[pl.ds(p, 128, stride=8), :])
            pp_hi[:, tile(p)] = hi
            pp_lo[:, tile(p)] = lo

    def lane_splitting():
        for j in range(5):
            for c in range(5):
                for a in range(10):
                    x[j, c * 100 + a * 10 : c * 100 + a * 10 + 10, :] = les[c, a, :, tile(j)]
            for a in range(5):
                for r in range(5):
                    i = a * 5 + r
                    x[j, APE + 4 * i : APE + 4 * i + 4, :] = ac[a, r, :, tile(j)]
                    x[j, APE_MV + 3 * i : APE_MV + 3 * i + 3, :] = mv[a, r, :, tile(j)]
                x[j, APE_DEN + 8 * a : APE_DEN + 8 * a + 5, :] = den[a, :, tile(j)]
                x[j, APE_SND + 8 * a : APE_SND + 8 * a + 5, :] = snd[a, :, tile(j)]
        value = relane(wide(x), perm[...])
        for j in range(5):
            y[j] = value[:, tile(j)]

    def les_rows_pass():
        lane = lax.broadcasted_iota(jnp.int32, (8, 128), 1)

        @pl.loop(0, 20)
        def _(t):
            er = t // 10
            base = (t - er * 10) * 10 + er * 5
            rows = pl.ds(pl.multiple_of(t * 8, 8), 8)
            q = [[y[j, pl.ds(c * 100 + base, 8), :] for j in range(5)] for c in range(5)]
            rec, v, p = [], [[], [], []], []
            for j in range(5):
                rec_j, v_j, p_j = les_prims([q[c][j] for c in range(5)])
                rec.append(rec_j)
                p.append(p_j)
                for k in range(3):
                    v[k].append(v_j[k])
                    vel[k, j, rows, :] = v_j[k]
                vel[3, j, rows, :] = p_j
            coefs = [coef[er, k] for k in range(5)]
            flux = [les_flux([q[c][j] for c in range(5)], [v[k][j] for k in range(3)], p[j], 2) for j in range(5)]
            s_left = les_speed(rec[4], [v[k][4] for k in range(3)], p[4], 2)
            s_right = pltpu.roll(les_speed(rec[0], [v[k][0] for k in range(3)], p[0], 2), 127, 1)
            half = 0.5 * jnp.maximum(s_left, s_right)
            for n in range(5):
                fr = pltpu.roll(flux[0][n], 127, 1)
                qr = pltpu.roll(q[n][0], 127, 1)
                h = 0.5 * (flux[4][n] + fr) - half * (qr - q[n][4])
                out = apply5([flux[j][n] for j in range(5)], T)
                out[4] = out[4] - LIFT * jnp.where(lane < 127, h, flux[4][n])
                out[0] = out[0] + LIFT * jnp.where(lane > 0, pltpu.roll(h, 1, 1), flux[0][n])
                for j in range(5):
                    f = les_flux([q[c][j] for c in range(5)], [v[k][j] for k in range(3)], p[j], 1)[n]
                    acc[j, pl.ds(n * 100 + base, 5), :] = (out[j] + radial(f, coefs))[0:5]
            dcoefs = [coef[2, k] for k in range(5)]
            d2v0 = apply5(v[0], D)
            d2v1 = apply5(v[1], D)
            for j in range(5):
                omega[0, j, rows, :] = radial(v[2][j], dcoefs) - d2v1[j]
                omega[1, j, rows, :] = d2v0[j]
                omega[2, j, rows, :] = -radial(v[0][j], dcoefs)

    def les_azimuth_pass():
        for c in range(3):
            for i in range(4):
                rt[i, c * 128 + 120 : c * 128 + 128, :] = jnp.zeros((8, 128), F32)

        @pl.loop(0, 2)
        def _(er):
            for j in range(5):
                at = [pl.ds(pl.multiple_of(er * 80 + a * 8, 8), 8) for a in range(10)]
                q = [[y[j, pl.ds(c * 100 + a * 10 + er * 5, 8), :] for a in range(10)] for c in range(5)]
                v = [[vel[k, j, at[a], :] for a in range(10)] for k in range(3)]
                p = [vel[3, j, at[a], :] for a in range(10)]
                flux = [les_flux([q[c][a] for c in range(5)], [v[k][a] for k in range(3)], p[a], 0) for a in range(10)]
                speed = [jnp.abs(v[0][a]) + jnp.sqrt(GAMMA * p[a] / q[0][a]) for a in (4, 5)]
                h = common(flux[4], flux[5], speed[0], speed[1], [q[c][4] for c in range(5)], [q[c][5] for c in range(5)])
                for n in range(5):
                    low = apply5([flux[a][n] for a in range(5)], T)
                    low[0] = low[0] + LIFT * flux[0][n]
                    low[4] = low[4] - LIFT * h[n]
                    top = apply5([flux[5 + a][n] for a in range(5)], T)
                    top[0] = top[0] + LIFT * h[n]
                    top[4] = top[4] - LIFT * flux[9][n]
                    for a, value in enumerate(low + top):
                        to = pl.ds(n * 100 + a * 10 + er * 5, 5)
                        acc[j, to, :] = acc[j, to, :] + value[0:5]
                for ea in range(2):
                    d0v1 = apply5([v[1][5 * ea + i] for i in range(5)], D)
                    d0v2 = apply5([v[2][5 * ea + i] for i in range(5)], D)
                    for i in range(5):
                        a = 5 * ea + i
                        w0 = omega[0, j, at[a], :]
                        w1 = omega[1, j, at[a], :] - d0v2[i]
                        w2 = omega[2, j, at[a], :] + d0v1[i]
                        lamb = [
                            w1 * v[2][a] - w2 * v[1][a],
                            w2 * v[0][a] - w0 * v[2][a],
                            w0 * v[1][a] - w1 * v[0][a],
                        ]
                        for c in range(3):
                            rt[2 * ea + er, pl.ds(c * 128 + i * 25 + j, 5, stride=5), :] = lamb[c][0:5]
        for i in range(4):
            hi, lo = split(rt[i])
            lamb_out[0:384, tile(i)] = hi
            lamb_out[384:768, tile(i)] = lo

    def les_radial_face():
        for j in range(5):
            left = [pl.ds(c * 100 + 4, 10, stride=10) for c in range(5)]
            right = [pl.ds(c * 100 + 5, 10, stride=10) for c in range(5)]
            h, _, _ = les_common([y[j, at, :] for at in left], [y[j, at, :] for at in right], 1)
            for n in range(5):
                acc[j, left[n], :] = acc[j, left[n], :] - LIFT * h[n]
                acc[j, right[n], :] = acc[j, right[n], :] + LIFT * h[n]
            acc[j, 500:512, :] = jnp.zeros((12, 128), F32)

    def acoustic():
        lane5 = lax.broadcasted_iota(jnp.int32, (5, 128), 1)
        state = [[None] * 5 for _ in range(5)]
        for a in range(5):
            for j in range(5):
                state[a][j] = (
                    [y[j, pl.ds(APE + a * 20 + c, 5, stride=4), :] for c in range(4)]
                    + [y[j, base + a * 8 : base + a * 8 + 5, :] for base in (APE_DEN, APE_SND)]
                    + [y[j, pl.ds(APE_MV + a * 15 + k, 5, stride=3), :] for k in range(3)]
                )
        carried = [[ape_carried(state[a][j]) for j in range(5)] for a in range(5)]
        lead = [[[ape_leading(state[a][j], k) for j in range(5)] for a in range(5)] for k in range(3)]
        total = [[[None] * 5 for _ in range(5)] for _ in range(4)]
        minus = -D
        mcoefs = [coef[3, k, 0:5] for k in range(5)]
        for j in range(5):
            first = apply5([lead[0][a][j] for a in range(5)], minus)
            other = apply5([carried[a][j] for a in range(5)], minus)
            for a in range(5):
                total[0][a][j] = first[a] + radial(lead[1][a][j], mcoefs)
                total[1][a][j] = other[a]
                total[2][a][j] = radial(carried[a][j], mcoefs)
        for a in range(5):
            first = apply5(lead[2][a], T)
            other = apply5(carried[a], T)
            shift = [pltpu.roll(jnp.pad(v, ((0, 3), (0, 0))), 127, 1)[0:5] for v in state[a][0]]
            h, fl, fr = ape_common(state[a][4], shift, 2)
            for n in range(4):
                own4 = lead[2][a][4] if n == 0 else carried[a][4] if n == 3 else jnp.zeros_like(carried[a][4])
                own0 = lead[2][a][0] if n == 0 else carried[a][0] if n == 3 else jnp.zeros_like(carried[a][0])
                back = pltpu.roll(jnp.pad(h[n], ((0, 3), (0, 0))), 1, 1)[0:5]
                lift4 = -LIFT * jnp.where(lane5 < 127, h[n], own4)
                lift0 = LIFT * jnp.where(lane5 > 0, back, own0)
                for j in range(5):
                    value = total[n][a][j]
                    if n in (0, 3):
                        extra = first[j] if n == 0 else other[j]
                        value = extra if value is None else value + extra
                    if j == 4:
                        value = value + lift4
                    if j == 0:
                        value = value + lift0
                    if value is None:
                        value = jnp.zeros((5, 128), F32)
                    da[j, pl.ds(a * 20 + n, 5, stride=4), :] = value
        for j in range(5):
            da[j, 100:104, :] = jnp.zeros((4, 128), F32)

    for part in (
        list_matrices, projection_matrices, lane_splitting, les_rows_pass, les_azimuth_pass, les_radial_face, acoustic,
    ):
        part()


def ape_face(buf, base, j):
    return [buf[j, base + 5 * n : base + 5 * n + 5, :] for n in range(9)]


def back_face(buf, j):
    rho = buf[j, 150:160, :]
    return [rho] + [rho * buf[j, c * 50 : c * 50 + 10, :] for c in range(3)] + [buf[j, 160:170, :]]


def les_rows(buf, j):
    return [buf[j, c * 10 : c * 10 + 10, :] for c in range(5)]


def les_common(ql, qr, k):
    rl, vl, pl_ = les_prims(ql)
    rr, vr, pr = les_prims(qr)
    fl, fr = les_flux(ql, vl, pl_, k), les_flux(qr, vr, pr, k)
    return common(fl, fr, les_speed(rl, vl, pl_, k), les_speed(rr, vr, pr, k), ql, qr), fl, fr


def finish_kernel(
    les, ac, acc, da_in, lamb_own, m, pp_hi, pp_lo, back, fwd, low, high, axial,
    fwd_in, low_in, high_in, axial_in, back_in, perm, perm_t, coef,
    les_out, ac_out, delta, result, yn, rt, rhs_hi, rhs_lo, osc, da, sem,
):
    rad = lax.axis_index("rad")
    first_half = lax.axis_index("group") == 0
    at_low, at_high = rad == 0, rad == lax.axis_size("rad") - 1

    def les_faces():
        value = relane(wide(acc), perm_t[...])
        for j in range(5):
            delta[j] = value[:, tile(j)]
        for j in range(5):
            own_low, own_high = les_rows(low, j), les_rows(high, j)
            nbr_low = [jnp.where(at_low, o, n) for o, n in zip(own_low, les_rows(low_in, j))]
            nbr_high = [jnp.where(at_high, o, n) for o, n in zip(own_high, les_rows(high_in, j))]
            h, _, fr = les_common(nbr_low, own_low, 1)
            g, fl, _ = les_common(own_high, nbr_high, 1)
            for n in range(5):
                at = pl.ds(n * 100, 10, stride=10)
                delta[j, at, :] = delta[j, at, :] + LIFT * (h[n] - fr[n])
                at = pl.ds(n * 100 + 9, 10, stride=10)
                delta[j, at, :] = delta[j, at, :] + LIFT * (fl[n] - g[n])
            h, _, fr = les_common(les_rows(fwd_in, j), back_face(back, j), 0)
            g, fl, _ = les_common(les_rows(fwd, j), back_face(back_in, j), 0)
            for n in range(5):
                at = slice(n * 100, n * 100 + 10)
                delta[j, at, :] = delta[j, at, :] + LIFT * (h[n] - fr[n])
                at = slice(n * 100 + 90, n * 100 + 100)
                delta[j, at, :] = delta[j, at, :] + LIFT * (fl[n] - g[n])
        own = [axial[16 * c : 16 * c + 16, :] for c in range(5)]
        nbr = [axial_in[16 * c : 16 * c + 16, :] for c in range(5)]
        ql = [jnp.where(first_half, o, n) for o, n in zip(own, nbr)]
        qr = [jnp.where(first_half, n, o) for o, n in zip(own, nbr)]
        h, fl, fr = les_common(ql, qr, 2)
        lane = lax.broadcasted_iota(jnp.int32, (10, 128), 1)
        on_last = (lane == 127) & first_half
        on_first = (lane == 0) & jnp.logical_not(first_half)
        for n in range(5):
            axis = LIFT * jnp.where(first_half, fl[n] - h[n], h[n] - fr[n])
            for a in range(10):
                column = jnp.broadcast_to(axis[0:10, a : a + 1], (10, 128))
                at = slice(n * 100 + a * 10, n * 100 + a * 10 + 10)
                for j in range(5):
                    value = delta[j, at, :]
                    if j == 0:
                        value = value + jnp.where(on_first, column, 0.0)
                    if j == 4:
                        value = value + jnp.where(on_last, column, 0.0)
                    result[n, a, :, tile(j)] = les[n, a, :, tile(j)] + DT * value
        pltpu.make_async_copy(result, les_out, sem).start()

    def sources():
        value = relane(jnp.concatenate([back_in[j, 0:160, :] for j in range(5)], axis=1), perm[...])
        for j in range(5):
            yn[j] = value[:, tile(j)]
        for c in range(3):
            for i in range(2):
                rt[i, c * 128 + 120 : c * 128 + 128, :] = jnp.zeros((8, 128), F32)
        dcoefs = [coef[2, k] for k in range(5)]
        for er in range(2):
            v = [[[None] * 5 for _ in range(5)] for _ in range(3)]
            for c in range(3):
                for a in range(5):
                    at = c * 50 + a * 10 + er * 5
                    v[c][a] = [yn[j, at : at + 8, :] for j in range(5)]
            d2v0 = [apply5(v[0][a], D) for a in range(5)]
            d2v1 = [apply5(v[1][a], D) for a in range(5)]
            for j in range(5):
                d0v1 = apply5([v[1][a][j] for a in range(5)], D)
                d0v2 = apply5([v[2][a][j] for a in range(5)], D)
                for a in range(5):
                    w0 = radial(v[2][a][j], dcoefs) - d2v1[a][j]
                    w1 = d2v0[a][j] - d0v2[a]
                    w2 = d0v1[a] - radial(v[0][a][j], dcoefs)
                    lamb = [
                        w1 * v[2][a][j] - w2 * v[1][a][j],
                        w2 * v[0][a][j] - w0 * v[2][a][j],
                        w0 * v[1][a][j] - w1 * v[0][a][j],
                    ]
                    for c in range(3):
                        rt[er, pl.ds(c * 128 + a * 25 + j, 5, stride=5), :] = lamb[c][0:5]
        near = jnp.concatenate(split(wide(rt)), axis=0)
        s = dot(jnp.concatenate([lamb_own[...], near], axis=1), m[...])
        s = s[0:384] + s[384:768]
        for p in range(8):
            for c in range(3):
                hi, lo = split(s[c * 128 : c * 128 + 128, tile(p)])
                rhs_hi[p * 128 : p * 128 + 128, tile(c)] = hi
                rhs_lo[p * 128 : p * 128 + 128, tile(c)] = lo
        hi = rhs_hi[...]
        out = dot(pp_hi[...], hi) + (dot(pp_lo[...], hi) + dot(pp_hi[...], rhs_lo[...]))
        for c in range(3):
            osc[c] = out[:, tile(c)]

    def acoustic():
        for j in range(5):
            da[j] = da_in[j]
            for a in range(5):
                for n in range(1, 4):
                    at = pl.ds(a * 20 + n, 5, stride=4)
                    da[j, at, :] = da[j, at, :] - osc[n - 1, pl.ds(a * 25 + j, 5, stride=5), :]
        value = relane(wide(da), perm_t[...])

        def axial_state(buf):
            def spread(base):
                rows = buf[base : base + 8, :]
                row = lax.broadcasted_iota(jnp.int32, (8, 128), 0)
                lanes = lax.broadcasted_iota(jnp.int32, (8, 128), 1)
                out = jnp.zeros((8, 128), F32)
                for a in range(5):
                    here = (lanes == a * 5 + row) & (row < 5)
                    out = jnp.where(here, jnp.broadcast_to(rows[:, a : a + 1], (8, 128)), out)
                return jnp.sum(out, axis=0, keepdims=True)

            used = lax.broadcasted_iota(jnp.int32, (1, 128), 1) < 25
            return (
                [buf[80 + c : 81 + c, :] for c in range(4)]
                + [jnp.where(used, spread(88), 1.0), spread(96)]
                + [buf[84 + k : 85 + k, :] for k in range(3)]
            )

        own, nbr = axial_state(axial), axial_state(axial_in)
        ql = [jnp.where(first_half, o, n) for o, n in zip(own, nbr)]
        qr = [jnp.where(first_half, n, o) for o, n in zip(own, nbr)]
        h, fl, fr = ape_common(ql, qr, 2)
        rows = []
        for n in range(4):
            fl_n = fl[0] if n == 0 else fl[1] if n == 3 else 0.0
            fr_n = fr[0] if n == 0 else fr[1] if n == 3 else 0.0
            rows.append(LIFT * jnp.where(first_half, fl_n - h[n], h[n] - fr_n))
        axis = jnp.concatenate(rows, axis=0)
        lane4 = lax.broadcasted_iota(jnp.int32, (4, 128), 1)
        on_last = (lane4 == 127) & first_half
        on_first = (lane4 == 0) & jnp.logical_not(first_half)
        for j in range(5):
            da[j] = value[:, tile(j)]

            def add(start, stride, h, own, k, sign):
                for n in range(4):
                    own_n = own[0] if n == 0 else own[1] if n == 1 + k else 0.0
                    at = pl.ds(start + n, 5, stride=stride)
                    da[j, at, :] = da[j, at, :] + sign * LIFT * (h[n] - own_n)

            h, _, fr = ape_common(ape_face(fwd_in, F_APE, j), ape_face(back, B_APE, j), 0)
            add(0, 4, h, fr, 0, 1.0)
            h, fl, _ = ape_common(ape_face(fwd, F_APE, j), ape_face(back_in, B_APE, j), 0)
            add(80, 4, h, fl, 0, -1.0)
            own_l, own_h = ape_face(low, F_APE, j), ape_face(high, F_APE, j)
            nbr_l = [jnp.where(at_low, o, n) for o, n in zip(own_l, ape_face(low_in, F_APE, j))]
            nbr_h = [jnp.where(at_high, o, n) for o, n in zip(own_h, ape_face(high_in, F_APE, j))]
            h, _, fr = ape_common(nbr_l, own_l, 1)
            add(0, 20, h, fr, 1, 1.0)
            h, fl, _ = ape_common(own_h, nbr_h, 1)
            add(16, 20, h, fl, 1, -1.0)
            for a in range(5):
                for r in range(5):
                    i = a * 5 + r
                    change = da[j, 4 * i : 4 * i + 4, :]
                    if j == 0 or j == 4:
                        column = jnp.broadcast_to(axis[:, i : i + 1], (4, 128))
                        change = change + jnp.where(on_last if j == 4 else on_first, column, 0.0)
                    ac_out[a, r, :, tile(j)] = ac[a, r, :, tile(j)] + DT * change

    les_faces()
    sources()
    acoustic()
    pltpu.make_async_copy(result, les_out, sem).wait()


def shape(*dims, dtype=F32):
    return jax.ShapeDtypeStruct(dims, dtype)


def cost(flops, size):
    return pl.CostEstimate(flops=flops, bytes_accessed=size, transcendentals=0)


def params():
    return pltpu.CompilerParams(vmem_limit_bytes=VMEM_LIMIT)


def body(les, ac, den, snd, mv, proj, counts, elem, pattern):
    vmem = pl.BlockSpec(memory_space=pltpu.VMEM)
    ac = jnp.transpose(ac, (1, 2, 0, 3))
    mv = jnp.transpose(mv, (1, 2, 0, 3))
    proj = jnp.transpose(proj, (1, 0, 2)).reshape(1000, 125)
    counts, elem, pattern = counts.reshape(1, 128), elem.reshape(1, 768), pattern.reshape(1, 768)
    perm = jnp.asarray(lane_split(), BF16)
    perm_t = jnp.asarray(lane_split().T, BF16)
    coef = jnp.asarray(radial_coefs(), F32)

    hbm = pl.BlockSpec(memory_space=pltpu.HBM)
    held = [pltpu.VMEM(a.shape, F32) for a in (les, ac, den, snd, mv)]
    back, fwd, low, high, axial, les, ac, den, snd, mv = pl.pallas_call(
        pack_kernel,
        out_shape=[pltpu.VMEM((5, n, 128), F32) for n in (B_ROWS, F_ROWS, F_ROWS, F_ROWS)]
        + [pltpu.VMEM((G_ROWS, 128), F32)]
        + held,
        in_specs=[hbm] * 5,
        out_specs=[vmem] * 10,
        scratch_shapes=[pltpu.SemaphoreType.DMA((9,))],
        compiler_params=params(),
        cost_estimate=cost(1_000_000, 5_000_000),
        name="pack",
    )(*[pltpu.with_memory_space_constraint(a, pltpu.HBM) for a in (les, ac, den, snd, mv)])

    azim, radc = lax.axis_size("azim"), lax.axis_size("rad")
    back_in = lax.ppermute(back, "azim", [(i, (i - 1) % azim) for i in range(azim)])
    fwd_in = lax.ppermute(fwd, "azim", [(i, (i + 1) % azim) for i in range(azim)])
    high_in = lax.ppermute(low, "rad", [(i, i - 1) for i in range(1, radc)])
    low_in = lax.ppermute(high, "rad", [(i, i + 1) for i in range(radc - 1)])
    axial_in = lax.ppermute(axial, "group", [(0, 1), (1, 0)])

    acc, da, lamb, m, pp_hi, pp_lo = pl.pallas_call(
        interior_kernel,
        out_shape=[
            shape(5, 512, 128), shape(5, 104, 128), shape(768, 512, dtype=BF16), shape(768, 1024, dtype=BF16),
            shape(128, 1024, dtype=BF16), shape(128, 1024, dtype=BF16),
        ],
        in_specs=[vmem] * 11,
        out_specs=[vmem] * 6,
        scratch_shapes=[
            pltpu.VMEM((5, ROWS, 128), F32),
            pltpu.VMEM((5, ROWS, 128), F32),
            pltpu.VMEM((4, 5, 160, 128), F32),
            pltpu.VMEM((3, 5, 160, 128), F32),
            pltpu.VMEM((4, 384, 128), F32),
            pltpu.VMEM((768, 768), BF16),
            pltpu.VMEM((1024, 768), BF16),
            pltpu.VMEM((1024, 128), F32),
        ],
        compiler_params=params(),
        cost_estimate=cost(5_000_000_000, 10_000_000),
        name="interior",
    )(les, ac, den, snd, mv, proj, counts, elem, pattern, perm, coef)

    les_next, ac_next = pl.pallas_call(
        finish_kernel,
        out_shape=[shape(5, 10, 10, NX), shape(5, 5, 4, NX)],
        in_specs=[vmem] * 21,
        out_specs=[hbm, vmem],
        scratch_shapes=[
            pltpu.VMEM((5, 512, 128), F32),
            pltpu.VMEM((5, 10, 10, NX), F32),
            pltpu.VMEM((5, 160, 128), F32),
            pltpu.VMEM((2, 384, 128), F32),
            pltpu.VMEM((1024, 384), BF16),
            pltpu.VMEM((1024, 384), BF16),
            pltpu.VMEM((3, 128, 128), F32),
            pltpu.VMEM((5, 104, 128), F32),
            pltpu.SemaphoreType.DMA(()),
        ],
        compiler_params=params(),
        cost_estimate=cost(500_000_000, 4_000_000),
        name="finish",
    )(
        les, ac, acc, da, lamb, m, pp_hi, pp_lo, back, fwd, low, high, axial,
        fwd_in, low_in, high_in, axial_in, back_in, perm, perm_t, coef,
    )
    return les_next, jnp.transpose(ac_next, (2, 0, 1, 3))


def solution(mesh):
    field = P(None, "azim", "rad", "group")
    node = P("azim", "rad", "group")
    lists = P("azim", "rad", "group", None)
    return jax.shard_map(
        body,
        mesh=mesh,
        in_specs=(field, field, node, node, field, P(), lists, lists, lists),
        out_specs=(field, field),
        check_vma=False,
    )
```

```python
import functools
import math

import jax
import jax.numpy as jnp
import numpy as np
from jax import lax
from jax.experimental import pallas as pl
from jax.experimental.pallas import tpu as pltpu
from jax.sharding import PartitionSpec as P

GAMMA = 1.4
DT = 0.05
LIFT = 10.0
F32 = jnp.float32
BF16 = jnp.bfloat16
NX = 640
NE = 128
VMEM_LIMIT = 40 * 1024 * 1024


def derivative_matrix():
    points = np.array([-1.0, -math.sqrt(3.0 / 7.0), 0.0, math.sqrt(3.0 / 7.0), 1.0])
    weights = np.array([1.0 / np.prod([points[j] - points[k] for k in range(5) if k != j]) for j in range(5)])
    matrix = np.zeros((5, 5))
    for i in range(5):
        for j in range(5):
            if i != j:
                matrix[i, j] = weights[j] / weights[i] / (points[i] - points[j])
        matrix[i, i] = -np.sum(matrix[i])
    return matrix


D = derivative_matrix()
T = -D.copy()
T[0, 0] -= LIFT
T[4, 4] += LIFT


def lane_split():
    p = np.zeros((NX, NX), np.float32)
    for e in range(NE):
        for j in range(5):
            p[5 * e + j, NE * j + e] = 1.0
    return p


def radial_coefs():
    inner, outer = T.copy(), T.copy()
    inner[0, 0] += LIFT
    outer[4, 4] -= LIFT
    out = np.zeros((4, 5, 8, 128), np.float32)
    for kind, m in enumerate((inner, outer, D, -D)):
        for k in range(5):
            out[kind, k, :5, :] = m[:, k][:, None]
    return out


def apply5(f, m):
    s = [f[0] + f[4], f[1] + f[3]]
    d = [f[0] - f[4], f[1] - f[3]]
    out = [None] * 5
    for i in range(2):
        even = (0.5 * (m[i, 0] + m[i, 4])) * s[0] + (0.5 * (m[i, 1] + m[i, 3])) * s[1] + m[i, 2] * f[2]
        odd = (0.5 * (m[i, 0] - m[i, 4])) * d[0] + (0.5 * (m[i, 1] - m[i, 3])) * d[1]
        out[i] = odd + even
        out[4 - i] = odd - even
    out[2] = (0.5 * (m[2, 0] - m[2, 4])) * d[0] + (0.5 * (m[2, 1] - m[2, 3])) * d[1]
    return out


def radial(f, coefs):
    total = coefs[0] * f[0:1, :]
    for k in range(1, 5):
        total = total + coefs[k] * f[k : k + 1, :]
    return total


def tile(j):
    return slice(NE * j, NE * j + NE)


def wide(ref):
    return jnp.concatenate([ref[j] for j in range(ref.shape[0])], axis=1)


def split(x):
    hi = x.astype(BF16)
    return hi, (x - hi.astype(F32)).astype(BF16)


def dot(a, b):
    return jnp.dot(a, b, preferred_element_type=F32)


def relane(x, matrix):
    return dot(jnp.concatenate(split(x), axis=1), matrix)


def les_prims(q):
    rec = 1.0 / q[0]
    v = [q[1] * rec, q[2] * rec, q[3] * rec]
    p = 0.4 * (q[4] - 0.5 * (q[1] * v[0] + q[2] * v[1] + q[3] * v[2]))
    return rec, v, p


def les_flux(q, v, p, k):
    out = [q[1 + k]]
    for j in range(3):
        out.append(q[1 + j] * v[k] + p if j == k else q[1 + j] * v[k])
    out.append((q[4] + p) * v[k])
    return out


def les_speed(rec, v, p, k):
    return jnp.abs(v[k]) + jnp.sqrt(GAMMA * p * rec)


def common(fl, fr, sl, sr, ql, qr):
    half = 0.5 * jnp.maximum(sl, sr)
    return [0.5 * (fl[n] + fr[n]) - half * (qr[n] - ql[n]) for n in range(len(fl))]


def ape_carried(s):
    return s[6] * s[1] + s[7] * s[2] + s[8] * s[3] + s[0] / s[4]


def ape_leading(s, k):
    return s[5] * s[5] * s[4] * s[1 + k] + s[6 + k] * s[0]


def ape_common(l, r, k, fl=None, fr=None):
    if fl is None:
        fl = (ape_leading(l, k), ape_carried(l))
    if fr is None:
        fr = (ape_leading(r, k), ape_carried(r))
    half = 0.5 * jnp.maximum(jnp.abs(l[6 + k]) + l[5], jnp.abs(r[6 + k]) + r[5])
    out = []
    for n in range(4):
        value = -half * (r[n] - l[n])
        if n == 0:
            value = value + 0.5 * (fl[0] + fr[0])
        elif n == 1 + k:
            value = value + 0.5 * (fl[1] + fr[1])
        out.append(value)
    return out, fl, fr


B_ROWS, F_ROWS, G_ROWS = 224, 96, 160
B_APE = 176
F_APE = 50


def pack_kernel(
    les_h, ac_h, den_h, snd_h, mv_h, back, fwd, inner, outer, axial, les, ac, den, snd, mv, sems,
):
    halves = [slice(0, 5), slice(5, 10)]
    copies = [[], [], []]
    for h in range(2):
        for c in range(5):
            copies[h].append(pltpu.make_async_copy(les_h.at[c, halves[h]], les.at[c, halves[h]], sems.at[5 * h + c]))
    for i, (src, dst) in enumerate(((ac_h, ac), (den_h, den), (snd_h, snd), (mv_h, mv))):
        copies[2].append(pltpu.make_async_copy(src, dst, sems.at[10 + i]))
    for group in (0, 2, 1):
        for copy in copies[group]:
            copy.start()
    even = lax.rem(lax.axis_index("rad"), 2) == 0

    def radial_faces(layers):
        for j in range(5):
            for c in range(5):
                for a in layers:
                    first, last = les[c, a, 0:1, tile(j)], les[c, a, 9:10, tile(j)]
                    inner[j, c * 10 + a : c * 10 + a + 1, :] = jnp.where(even, last, first)
                    outer[j, c * 10 + a : c * 10 + a + 1, :] = jnp.where(even, first, last)

    for copy in copies[0]:
        copy.wait()
    for a in range(5):
        rec = 1.0 / les[0, a]
        for c in range(3):
            v = les[1 + c, a] * rec
            for j in range(5):
                back[j, c * 50 + a * 10 : c * 50 + a * 10 + 10, :] = v[:, tile(j)]
    for j in range(5):
        back[j, 150:160, :] = les[0, 0, :, tile(j)]
        back[j, 160:170, :] = les[4, 0, :, tile(j)]
        back[j, 170:176, :] = jnp.zeros((6, 128), F32)
        back[j, 221:224, :] = jnp.zeros((3, 128), F32)
        for buf in (fwd, inner, outer):
            buf[j, 95:96, :] = jnp.zeros((1, 128), F32)
    radial_faces(range(5))
    for copy in copies[2]:
        copy.wait()
    for j in range(5):
        for buf, a, base in ((back, 0, B_APE), (fwd, 4, F_APE)):
            for r in range(5):
                buf[j, pl.ds(base + r, 4, stride=5), :] = ac[a, r, :, tile(j)]
                buf[j, pl.ds(base + 30 + r, 3, stride=5), :] = mv[a, r, :, tile(j)]
            buf[j, base + 20 : base + 25, :] = den[a, :, tile(j)]
            buf[j, base + 25 : base + 30, :] = snd[a, :, tile(j)]
        for a in range(5):
            for src, base in ((ac, F_APE), (mv, F_APE + 30)):
                first, last = src[a, 0, :, tile(j)], src[a, 4, :, tile(j)]
                at = pl.ds(base + a, first.shape[0], stride=5)
                inner[j, at, :] = jnp.where(even, last, first)
                outer[j, at, :] = jnp.where(even, first, last)
            for src, base in ((den, F_APE + 20), (snd, F_APE + 25)):
                first, last = src[a, 0:1, tile(j)], src[a, 4:5, tile(j)]
                inner[j, base + a : base + a + 1, :] = jnp.where(even, last, first)
                outer[j, base + a : base + a + 1, :] = jnp.where(even, first, last)
    for copy in copies[1]:
        copy.wait()
    for j in range(5):
        for c in range(5):
            fwd[j, c * 10 : c * 10 + 10, :] = les[c, 9, :, tile(j)]
    radial_faces(range(5, 10))
    first = lax.axis_index("group") == 0

    def end(ref, *at):
        return jnp.where(first, ref[(*at, slice(None), slice(NX - 1, NX))], ref[(*at, slice(None), slice(0, 1))])

    def gather(columns, rows):
        lane = lax.broadcasted_iota(jnp.int32, (rows, 128), 1)
        value = jnp.broadcast_to(columns[0], (rows, 128))
        for i in range(1, len(columns)):
            value = jnp.where(lane == i, jnp.broadcast_to(columns[i], (rows, 128)), value)
        return value

    for c in range(5):
        axial[16 * c : 16 * c + 10, :] = gather([end(les, c, a) for a in range(10)], 10)
        axial[16 * c + 10 : 16 * c + 16, :] = jnp.ones((6, 128), F32)
    axial[80:84, :] = gather([end(ac, a, r) for a in range(5) for r in range(5)], 4)
    axial[84:87, :] = gather([end(mv, a, r) for a in range(5) for r in range(5)], 3)
    axial[87:88, :] = jnp.zeros((1, 128), F32)
    axial[88:93, :] = gather([end(den, a) for a in range(5)], 5)
    axial[93:96, :] = jnp.zeros((3, 128), F32)
    axial[96:101, :] = gather([end(snd, a) for a in range(5)], 5)
    axial[101:160, :] = jnp.zeros((59, 128), F32)


ROWS = 768
APE, APE_MV, APE_DEN, APE_SND = 504, 608, 688, 728


def interior_kernel(
    les, ac, den, snd, mv, proj, counts, elem, pattern, perm, coef,
    acc, da, lamb_out, m_out, pp_hi, pp_lo,
    x, y, vel, omega, rt, one_hot, owned, flat,
):
    def list_matrices():
        upper = lax.broadcasted_iota(jnp.int32, (NE, NE), 1)
        lower = lax.broadcasted_iota(jnp.int32, (NE, NE), 0)
        row = jnp.broadcast_to(counts[...], (NE, NE)).astype(F32)
        ends = jnp.sum(jnp.where(upper <= lower, row, 0.0), axis=1, keepdims=True)
        starts = jnp.sum(jnp.where(upper < lower, row, 0.0), axis=1, keepdims=True)
        position = lax.broadcasted_iota(jnp.int32, (NE, 768), 1).astype(F32)
        mine = jnp.where((position >= starts) & (position < ends), jnp.broadcast_to(pattern[...], (NE, 768)), -1)
        for p in range(8):
            owned[p * NE : p * NE + NE, :] = jnp.where(mine == p, 1.0, 0.0).astype(BF16)
        source = jnp.broadcast_to(elem[...], (NE, 768))
        for i in range(6):
            which = lax.broadcasted_iota(jnp.int32, (NE, 768), 0) + i * NE
            one_hot[i * NE : i * NE + NE, :] = jnp.where(which == source, 1.0, 0.0).astype(BF16)
        m_out[...] = lax.dot_general(
            one_hot[...], owned[...], (((1,), (1,)), ((), ())), preferred_element_type=F32
        ).astype(BF16)

    def projection_matrices():
        flat[...] = jnp.zeros((1024, 128), F32)
        flat[0:1000, 0:125] = proj[...]
        for p in range(8):
            hi, lo = split(flat[pl.ds(p, 128, stride=8), :])
            pp_hi[:, tile(p)] = hi
            pp_lo[:, tile(p)] = lo

    def lane_splitting():
        for j in range(5):
            for c in range(5):
                for a in range(10):
                    x[j, c * 100 + a * 10 : c * 100 + a * 10 + 10, :] = les[c, a, :, tile(j)]
            for a in range(5):
                for r in range(5):
                    i = a * 5 + r
                    x[j, APE + 4 * i : APE + 4 * i + 4, :] = ac[a, r, :, tile(j)]
                    x[j, APE_MV + 3 * i : APE_MV + 3 * i + 3, :] = mv[a, r, :, tile(j)]
                x[j, APE_DEN + 8 * a : APE_DEN + 8 * a + 5, :] = den[a, :, tile(j)]
                x[j, APE_SND + 8 * a : APE_SND + 8 * a + 5, :] = snd[a, :, tile(j)]
        value = relane(wide(x), perm[...])
        for j in range(5):
            y[j] = value[:, tile(j)]

    def les_rows_pass():
        lane = lax.broadcasted_iota(jnp.int32, (8, 128), 1)

        @pl.loop(0, 20, unroll=5)
        def _(t):
            er = t // 10
            base = (t - er * 10) * 10 + er * 5
            rows = pl.ds(pl.multiple_of(t * 8, 8), 8)
            q = [[y[j, pl.ds(c * 100 + base, 8), :] for j in range(5)] for c in range(5)]
            rec, v, p = [], [[], [], []], []
            for j in range(5):
                rec_j, v_j, p_j = les_prims([q[c][j] for c in range(5)])
                rec.append(rec_j)
                p.append(p_j)
                for k in range(3):
                    v[k].append(v_j[k])
                    vel[k, j, rows, :] = v_j[k]
                vel[3, j, rows, :] = p_j
            coefs = [coef[er, k] for k in range(5)]
            flux = [les_flux([q[c][j] for c in range(5)], [v[k][j] for k in range(3)], p[j], 2) for j in range(5)]
            s_left = les_speed(rec[4], [v[k][4] for k in range(3)], p[4], 2)
            s_right = pltpu.roll(les_speed(rec[0], [v[k][0] for k in range(3)], p[0], 2), 127, 1)
            half = 0.5 * jnp.maximum(s_left, s_right)
            for n in range(5):
                fr = pltpu.roll(flux[0][n], 127, 1)
                qr = pltpu.roll(q[n][0], 127, 1)
                h = 0.5 * (flux[4][n] + fr) - half * (qr - q[n][4])
                out = apply5([flux[j][n] for j in range(5)], T)
                out[4] = out[4] - LIFT * jnp.where(lane < 127, h, flux[4][n])
                out[0] = out[0] + LIFT * jnp.where(lane > 0, pltpu.roll(h, 1, 1), flux[0][n])
                for j in range(5):
                    f = les_flux([q[c][j] for c in range(5)], [v[k][j] for k in range(3)], p[j], 1)[n]
                    acc[j, pl.ds(n * 100 + base, 5), :] = (out[j] + radial(f, coefs))[0:5]
            dcoefs = [coef[2, k] for k in range(5)]
            d2v0 = apply5(v[0], D)
            d2v1 = apply5(v[1], D)
            for j in range(5):
                omega[0, j, rows, :] = radial(v[2][j], dcoefs) - d2v1[j]
                omega[1, j, rows, :] = d2v0[j]
                omega[2, j, rows, :] = -radial(v[0][j], dcoefs)

    def les_azimuth_pass():
        for c in range(3):
            for i in range(4):
                rt[i, c * 128 + 120 : c * 128 + 128, :] = jnp.zeros((8, 128), F32)

        @pl.loop(0, 2)
        def _(er):
            for j in range(5):
                at = [pl.ds(pl.multiple_of(er * 80 + a * 8, 8), 8) for a in range(10)]
                q = [[y[j, pl.ds(c * 100 + a * 10 + er * 5, 8), :] for a in range(10)] for c in range(5)]
                v = [[vel[k, j, at[a], :] for a in range(10)] for k in range(3)]
                p = [vel[3, j, at[a], :] for a in range(10)]
                flux = [les_flux([q[c][a] for c in range(5)], [v[k][a] for k in range(3)], p[a], 0) for a in range(10)]
                speed = [jnp.abs(v[0][a]) + jnp.sqrt(GAMMA * p[a] / q[0][a]) for a in (4, 5)]
                h = common(flux[4], flux[5], speed[0], speed[1], [q[c][4] for c in range(5)], [q[c][5] for c in range(5)])
                for n in range(5):
                    low = apply5([flux[a][n] for a in range(5)], T)
                    low[0] = low[0] + LIFT * flux[0][n]
                    low[4] = low[4] - LIFT * h[n]
                    top = apply5([flux[5 + a][n] for a in range(5)], T)
                    top[0] = top[0] + LIFT * h[n]
                    top[4] = top[4] - LIFT * flux[9][n]
                    for a, value in enumerate(low + top):
                        to = pl.ds(n * 100 + a * 10 + er * 5, 5)
                        acc[j, to, :] = acc[j, to, :] + value[0:5]
                for ea in range(2):
                    d0v1 = apply5([v[1][5 * ea + i] for i in range(5)], D)
                    d0v2 = apply5([v[2][5 * ea + i] for i in range(5)], D)
                    for i in range(5):
                        a = 5 * ea + i
                        w0 = omega[0, j, at[a], :]
                        w1 = omega[1, j, at[a], :] - d0v2[i]
                        w2 = omega[2, j, at[a], :] + d0v1[i]
                        lamb = [
                            w1 * v[2][a] - w2 * v[1][a],
                            w2 * v[0][a] - w0 * v[2][a],
                            w0 * v[1][a] - w1 * v[0][a],
                        ]
                        for c in range(3):
                            rt[2 * ea + er, pl.ds(c * 128 + i * 25 + j, 5, stride=5), :] = lamb[c][0:5]
        for i in range(4):
            hi, lo = split(rt[i])
            lamb_out[0:384, tile(i)] = hi
            lamb_out[384:768, tile(i)] = lo

    def les_radial_face():
        for j in range(5):
            left = [pl.ds(c * 100 + 4, 10, stride=10) for c in range(5)]
            right = [pl.ds(c * 100 + 5, 10, stride=10) for c in range(5)]
            h, _, _ = les_common([y[j, at, :] for at in left], [y[j, at, :] for at in right], 1)
            for n in range(5):
                acc[j, left[n], :] = acc[j, left[n], :] - LIFT * h[n]
                acc[j, right[n], :] = acc[j, right[n], :] + LIFT * h[n]
            acc[j, 500:512, :] = jnp.zeros((12, 128), F32)

    def acoustic():
        lane5 = lax.broadcasted_iota(jnp.int32, (5, 128), 1)
        state = [[None] * 5 for _ in range(5)]
        for a in range(5):
            for j in range(5):
                state[a][j] = (
                    [y[j, pl.ds(APE + a * 20 + c, 5, stride=4), :] for c in range(4)]
                    + [y[j, base + a * 8 : base + a * 8 + 5, :] for base in (APE_DEN, APE_SND)]
                    + [y[j, pl.ds(APE_MV + a * 15 + k, 5, stride=3), :] for k in range(3)]
                )
        carried = [[ape_carried(state[a][j]) for j in range(5)] for a in range(5)]
        lead = [[[ape_leading(state[a][j], k) for j in range(5)] for a in range(5)] for k in range(3)]
        total = [[[None] * 5 for _ in range(5)] for _ in range(4)]
        minus = -D
        mcoefs = [coef[3, k, 0:5] for k in range(5)]
        for j in range(5):
            first = apply5([lead[0][a][j] for a in range(5)], minus)
            other = apply5([carried[a][j] for a in range(5)], minus)
            for a in range(5):
                total[0][a][j] = first[a] + radial(lead[1][a][j], mcoefs)
                total[1][a][j] = other[a]
                total[2][a][j] = radial(carried[a][j], mcoefs)
        for a in range(5):
            first = apply5(lead[2][a], T)
            other = apply5(carried[a], T)
            shift = [pltpu.roll(jnp.pad(v, ((0, 3), (0, 0))), 127, 1)[0:5] for v in state[a][0]]
            h, fl, fr = ape_common(state[a][4], shift, 2)
            for n in range(4):
                own4 = lead[2][a][4] if n == 0 else carried[a][4] if n == 3 else jnp.zeros_like(carried[a][4])
                own0 = lead[2][a][0] if n == 0 else carried[a][0] if n == 3 else jnp.zeros_like(carried[a][0])
                back = pltpu.roll(jnp.pad(h[n], ((0, 3), (0, 0))), 1, 1)[0:5]
                lift4 = -LIFT * jnp.where(lane5 < 127, h[n], own4)
                lift0 = LIFT * jnp.where(lane5 > 0, back, own0)
                for j in range(5):
                    value = total[n][a][j]
                    if n in (0, 3):
                        extra = first[j] if n == 0 else other[j]
                        value = extra if value is None else value + extra
                    if j == 4:
                        value = value + lift4
                    if j == 0:
                        value = value + lift0
                    if value is None:
                        value = jnp.zeros((5, 128), F32)
                    da[j, pl.ds(a * 20 + n, 5, stride=4), :] = value
        for j in range(5):
            da[j, 100:104, :] = jnp.zeros((4, 128), F32)

    for part in (
        list_matrices, projection_matrices, lane_splitting, les_rows_pass, les_azimuth_pass, les_radial_face, acoustic,
    ):
        part()


def ape_face(buf, base, j):
    return [buf[j, base + 5 * n : base + 5 * n + 5, :] for n in range(9)]


def back_face(buf, j):
    rho = buf[j, 150:160, :]
    return [rho] + [rho * buf[j, c * 50 : c * 50 + 10, :] for c in range(3)] + [buf[j, 160:170, :]]


def les_rows(buf, j):
    return [buf[j, c * 10 : c * 10 + 10, :] for c in range(5)]


def les_common(ql, qr, k):
    rl, vl, pl_ = les_prims(ql)
    rr, vr, pr = les_prims(qr)
    fl, fr = les_flux(ql, vl, pl_, k), les_flux(qr, vr, pr, k)
    return common(fl, fr, les_speed(rl, vl, pl_, k), les_speed(rr, vr, pr, k), ql, qr), fl, fr


def les_change(own, nbr, k, side):
    ro, vo, po = les_prims(own)
    rn, vn, pn = les_prims(nbr)
    fo, fn = les_flux(own, vo, po, k), les_flux(nbr, vn, pn, k)
    half = 0.5 * LIFT * jnp.maximum(les_speed(ro, vo, po, k), les_speed(rn, vn, pn, k))
    return [(0.5 * LIFT * side) * (fo[n] - fn[n]) + half * (nbr[n] - own[n]) for n in range(5)]


def ape_change(own, nbr, k, side):
    half = 0.5 * LIFT * jnp.maximum(jnp.abs(own[6 + k]) + own[5], jnp.abs(nbr[6 + k]) + nbr[5])
    out = [half * (nbr[n] - own[n]) for n in range(4)]
    out[0] = out[0] + (0.5 * LIFT * side) * (ape_leading(own, k) - ape_leading(nbr, k))
    out[1 + k] = out[1 + k] + (0.5 * LIFT * side) * (ape_carried(own) - ape_carried(nbr))
    return out


def finish_kernel(
    les, ac, acc, da_in, lamb_own, m, pp_hi, pp_lo, back, fwd, inner, outer, axial,
    fwd_in, inner_in, outer_in, axial_in, back_in, perm, perm_t, coef,
    les_out, ac_out, delta, result, yn, rt, rhs_hi, rhs_lo, osc, da, sem,
):
    rad = lax.axis_index("rad")
    even = lax.rem(rad, 2) == 0
    first_half = lax.axis_index("group") == 0
    inner_side, axis_side = jnp.where(even, 1.0, -1.0), jnp.where(first_half, 1.0, -1.0)
    inner_row = jnp.where(even, 9, 0)
    at_end = (rad == 0) | (rad == lax.axis_size("rad") - 1)

    def les_faces():
        value = relane(wide(acc), perm_t[...])
        for j in range(5):
            delta[j] = value[:, tile(j)]
        for j in range(5):

            def add(start, stride, change):
                for n in range(5):
                    at = pl.ds(n * 100 + start, 10, stride=stride)
                    delta[j, at, :] = delta[j, at, :] + change[n]

            add(inner_row, 10, les_change(les_rows(inner, j), les_rows(inner_in, j), 1, inner_side))
            own = les_rows(outer, j)
            nbr = [jnp.where(at_end, o, n) for o, n in zip(own, les_rows(outer_in, j))]
            add(9 - inner_row, 10, les_change(own, nbr, 1, -inner_side))
            add(0, 1, les_change(back_face(back, j), les_rows(fwd_in, j), 0, -1.0))
            add(90, 1, les_change(les_rows(fwd, j), back_face(back_in, j), 0, 1.0))
        own = [axial[16 * c : 16 * c + 16, :] for c in range(5)]
        nbr = [axial_in[16 * c : 16 * c + 16, :] for c in range(5)]
        change = les_change(own, nbr, 2, axis_side)
        lane = lax.broadcasted_iota(jnp.int32, (10, 128), 1)
        on_last = (lane == 127) & first_half
        on_first = (lane == 0) & jnp.logical_not(first_half)
        for n in range(5):
            for a in range(10):
                column = jnp.broadcast_to(change[n][0:10, a : a + 1], (10, 128))
                at = slice(n * 100 + a * 10, n * 100 + a * 10 + 10)
                for j in range(5):
                    value = delta[j, at, :]
                    if j == 0:
                        value = value + jnp.where(on_first, column, 0.0)
                    if j == 4:
                        value = value + jnp.where(on_last, column, 0.0)
                    result[n, a, :, tile(j)] = les[n, a, :, tile(j)] + DT * value

    def send_les():
        pltpu.make_async_copy(result, les_out, sem).start()

    def sources():
        value = relane(jnp.concatenate([back_in[j, 0:160, :] for j in range(5)], axis=1), perm[...])
        for j in range(5):
            yn[j] = value[:, tile(j)]
        for c in range(3):
            for i in range(2):
                rt[i, c * 128 + 120 : c * 128 + 128, :] = jnp.zeros((8, 128), F32)
        dcoefs = [coef[2, k] for k in range(5)]
        for er in range(2):
            v = [[[None] * 5 for _ in range(5)] for _ in range(3)]
            for c in range(3):
                for a in range(5):
                    at = c * 50 + a * 10 + er * 5
                    v[c][a] = [yn[j, at : at + 8, :] for j in range(5)]
            d2v0 = [apply5(v[0][a], D) for a in range(5)]
            d2v1 = [apply5(v[1][a], D) for a in range(5)]
            for j in range(5):
                d0v1 = apply5([v[1][a][j] for a in range(5)], D)
                d0v2 = apply5([v[2][a][j] for a in range(5)], D)
                for a in range(5):
                    w0 = radial(v[2][a][j], dcoefs) - d2v1[a][j]
                    w1 = d2v0[a][j] - d0v2[a]
                    w2 = d0v1[a] - radial(v[0][a][j], dcoefs)
                    lamb = [
                        w1 * v[2][a][j] - w2 * v[1][a][j],
                        w2 * v[0][a][j] - w0 * v[2][a][j],
                        w0 * v[1][a][j] - w1 * v[0][a][j],
                    ]
                    for c in range(3):
                        rt[er, pl.ds(c * 128 + a * 25 + j, 5, stride=5), :] = lamb[c][0:5]
        near = jnp.concatenate(split(wide(rt)), axis=0)
        s = dot(jnp.concatenate([lamb_own[...], near], axis=1), m[...])
        s = s[0:384] + s[384:768]
        for p in range(8):
            for c in range(3):
                hi, lo = split(s[c * 128 : c * 128 + 128, tile(p)])
                rhs_hi[p * 128 : p * 128 + 128, tile(c)] = hi
                rhs_lo[p * 128 : p * 128 + 128, tile(c)] = lo
        hi = rhs_hi[...]
        out = dot(pp_hi[...], hi) + (dot(pp_lo[...], hi) + dot(pp_hi[...], rhs_lo[...]))
        for c in range(3):
            osc[c] = out[:, tile(c)]

    def acoustic():
        for j in range(5):
            da[j] = da_in[j]
            for a in range(5):
                for n in range(1, 4):
                    at = pl.ds(a * 20 + n, 5, stride=4)
                    da[j, at, :] = da[j, at, :] - osc[n - 1, pl.ds(a * 25 + j, 5, stride=5), :]
        value = relane(wide(da), perm_t[...])

        def axial_state(buf):
            def spread(base):
                rows = buf[base : base + 8, :]
                row = lax.broadcasted_iota(jnp.int32, (8, 128), 0)
                lanes = lax.broadcasted_iota(jnp.int32, (8, 128), 1)
                out = jnp.zeros((8, 128), F32)
                for a in range(5):
                    here = (lanes == a * 5 + row) & (row < 5)
                    out = jnp.where(here, jnp.broadcast_to(rows[:, a : a + 1], (8, 128)), out)
                return jnp.sum(out, axis=0, keepdims=True)

            used = lax.broadcasted_iota(jnp.int32, (1, 128), 1) < 25
            return (
                [buf[80 + c : 81 + c, :] for c in range(4)]
                + [jnp.where(used, spread(88), 1.0), spread(96)]
                + [buf[84 + k : 85 + k, :] for k in range(3)]
            )

        own, nbr = axial_state(axial), axial_state(axial_in)
        axis = jnp.concatenate(ape_change(own, nbr, 2, axis_side), axis=0)
        lane4 = lax.broadcasted_iota(jnp.int32, (4, 128), 1)
        on_last = (lane4 == 127) & first_half
        on_first = (lane4 == 0) & jnp.logical_not(first_half)
        for j in range(5):
            da[j] = value[:, tile(j)]

            def add(start, stride, change):
                for n in range(4):
                    at = pl.ds(start + n, 5, stride=stride)
                    da[j, at, :] = da[j, at, :] + change[n]

            add(0, 4, ape_change(ape_face(back, B_APE, j), ape_face(fwd_in, F_APE, j), 0, -1.0))
            add(80, 4, ape_change(ape_face(fwd, F_APE, j), ape_face(back_in, B_APE, j), 0, 1.0))
            own, nbr = ape_face(inner, F_APE, j), ape_face(inner_in, F_APE, j)
            add(jnp.where(even, 16, 0), 20, ape_change(own, nbr, 1, inner_side))
            own = ape_face(outer, F_APE, j)
            nbr = [jnp.where(at_end, o, n) for o, n in zip(own, ape_face(outer_in, F_APE, j))]
            add(jnp.where(even, 0, 16), 20, ape_change(own, nbr, 1, -inner_side))
            for a in range(5):
                for r in range(5):
                    i = a * 5 + r
                    change = da[j, 4 * i : 4 * i + 4, :]
                    if j == 0 or j == 4:
                        column = jnp.broadcast_to(axis[:, i : i + 1], (4, 128))
                        change = change + jnp.where(on_last if j == 4 else on_first, column, 0.0)
                    ac_out[a, r, :, tile(j)] = ac[a, r, :, tile(j)] + DT * change

    for part in (les_faces, send_les, sources, acoustic):
        part()
    pltpu.make_async_copy(result, les_out, sem).wait()


def shape(*dims, dtype=F32):
    return jax.ShapeDtypeStruct(dims, dtype)


def cost(flops, size):
    return pl.CostEstimate(flops=flops, bytes_accessed=size, transcendentals=0)


def params():
    return pltpu.CompilerParams(vmem_limit_bytes=VMEM_LIMIT)


def body(les, ac, den, snd, mv, proj, counts, elem, pattern):
    vmem = pl.BlockSpec(memory_space=pltpu.VMEM)
    ac = jnp.transpose(ac, (1, 2, 0, 3))
    mv = jnp.transpose(mv, (1, 2, 0, 3))
    proj = jnp.transpose(proj, (1, 0, 2)).reshape(1000, 125)
    counts, elem, pattern = counts.reshape(1, 128), elem.reshape(1, 768), pattern.reshape(1, 768)
    perm = jnp.asarray(np.tile(lane_split(), (2, 1)), BF16)
    perm_t = jnp.asarray(np.tile(lane_split().T, (2, 1)), BF16)
    coef = jnp.asarray(radial_coefs(), F32)

    hbm = pl.BlockSpec(memory_space=pltpu.HBM)
    held = [pltpu.VMEM(a.shape, F32) for a in (les, ac, den, snd, mv)]
    back, fwd, inner, outer, axial, les, ac, den, snd, mv = pl.pallas_call(
        pack_kernel,
        out_shape=[pltpu.VMEM((5, n, 128), F32) for n in (B_ROWS, F_ROWS, F_ROWS, F_ROWS)]
        + [pltpu.VMEM((G_ROWS, 128), F32)]
        + held,
        in_specs=[hbm] * 5,
        out_specs=[vmem] * 10,
        scratch_shapes=[pltpu.SemaphoreType.DMA((14,))],
        compiler_params=params(),
        cost_estimate=cost(1_000_000, 5_000_000),
        name="pack",
    )(*[pltpu.with_memory_space_constraint(a, pltpu.HBM) for a in (les, ac, den, snd, mv)])

    azim, radc = lax.axis_size("azim"), lax.axis_size("rad")
    back_in = lax.ppermute(back, "azim", [(i, (i - 1) % azim) for i in range(azim)])
    fwd_in = lax.ppermute(fwd, "azim", [(i, (i + 1) % azim) for i in range(azim)])
    inner_in = lax.ppermute(inner, "rad", [(i, i ^ 1) for i in range(radc)])
    outer_in = lax.ppermute(outer, "rad", [p for i in range(1, radc - 1, 2) for p in ((i, i + 1), (i + 1, i))])
    axial_in = lax.ppermute(axial, "group", [(0, 1), (1, 0)])

    acc, da, lamb, m, pp_hi, pp_lo = pl.pallas_call(
        interior_kernel,
        out_shape=[
            shape(5, 512, 128), shape(5, 104, 128), shape(768, 512, dtype=BF16), shape(768, 1024, dtype=BF16),
            shape(128, 1024, dtype=BF16), shape(128, 1024, dtype=BF16),
        ],
        in_specs=[vmem] * 11,
        out_specs=[vmem] * 6,
        scratch_shapes=[
            pltpu.VMEM((5, ROWS, 128), F32),
            pltpu.VMEM((5, ROWS, 128), F32),
            pltpu.VMEM((4, 5, 160, 128), F32),
            pltpu.VMEM((3, 5, 160, 128), F32),
            pltpu.VMEM((4, 384, 128), F32),
            pltpu.VMEM((768, 768), BF16),
            pltpu.VMEM((1024, 768), BF16),
            pltpu.VMEM((1024, 128), F32),
        ],
        compiler_params=params(),
        cost_estimate=cost(5_000_000_000, 10_000_000),
        name="interior",
    )(les, ac, den, snd, mv, proj, counts, elem, pattern, perm, coef)

    les_next, ac_next = pl.pallas_call(
        finish_kernel,
        out_shape=[shape(5, 10, 10, NX), shape(5, 5, 4, NX)],
        in_specs=[vmem] * 21,
        out_specs=[hbm, vmem],
        scratch_shapes=[
            pltpu.VMEM((5, 512, 128), F32),
            pltpu.VMEM((5, 10, 10, NX), F32),
            pltpu.VMEM((5, 160, 128), F32),
            pltpu.VMEM((2, 384, 128), F32),
            pltpu.VMEM((1024, 384), BF16),
            pltpu.VMEM((1024, 384), BF16),
            pltpu.VMEM((3, 128, 128), F32),
            pltpu.VMEM((5, 104, 128), F32),
            pltpu.SemaphoreType.DMA(()),
        ],
        compiler_params=params(),
        cost_estimate=cost(500_000_000, 4_000_000),
        name="finish",
    )(
        les, ac, acc, da, lamb, m, pp_hi, pp_lo, back, fwd, inner, outer, axial,
        fwd_in, inner_in, outer_in, axial_in, back_in, perm, perm_t, coef,
    )
    return les_next, jnp.transpose(ac_next, (2, 0, 1, 3))


def solution(mesh):
    field = P(None, "azim", "rad", "group")
    node = P("azim", "rad", "group")
    lists = P("azim", "rad", "group", None)
    return jax.shard_map(
        body,
        mesh=mesh,
        in_specs=(field, field, node, node, field, P(), lists, lists, lists),
        out_specs=(field, field),
        check_vma=False,
    )
```

```python
import functools
import math

import jax
import jax.numpy as jnp
import numpy as np
from jax import lax
from jax.experimental import pallas as pl
from jax.experimental.pallas import tpu as pltpu
from jax.sharding import PartitionSpec as P

GAMMA = 1.4
DT = 0.05
LIFT = 10.0
F32 = jnp.float32
BF16 = jnp.bfloat16
NX = 640
NE = 128
VMEM_LIMIT = 40 * 1024 * 1024


def derivative_matrix():
    points = np.array([-1.0, -math.sqrt(3.0 / 7.0), 0.0, math.sqrt(3.0 / 7.0), 1.0])
    weights = np.array([1.0 / np.prod([points[j] - points[k] for k in range(5) if k != j]) for j in range(5)])
    matrix = np.zeros((5, 5))
    for i in range(5):
        for j in range(5):
            if i != j:
                matrix[i, j] = weights[j] / weights[i] / (points[i] - points[j])
        matrix[i, i] = -np.sum(matrix[i])
    return matrix


D = derivative_matrix()
T = -D.copy()
T[0, 0] -= LIFT
T[4, 4] += LIFT


def lane_split():
    p = np.zeros((NX, NX), np.float32)
    for e in range(NE):
        for j in range(5):
            p[5 * e + j, NE * j + e] = 1.0
    return p


def radial_coefs():
    inner, outer = T.copy(), T.copy()
    inner[0, 0] += LIFT
    outer[4, 4] -= LIFT
    out = np.zeros((4, 5, 8, 128), np.float32)
    for kind, m in enumerate((inner, outer, D, -D)):
        for k in range(5):
            out[kind, k, :5, :] = m[:, k][:, None]
    return out


def apply5(f, m):
    s = [f[0] + f[4], f[1] + f[3]]
    d = [f[0] - f[4], f[1] - f[3]]
    out = [None] * 5
    for i in range(2):
        even = (0.5 * (m[i, 0] + m[i, 4])) * s[0] + (0.5 * (m[i, 1] + m[i, 3])) * s[1] + m[i, 2] * f[2]
        odd = (0.5 * (m[i, 0] - m[i, 4])) * d[0] + (0.5 * (m[i, 1] - m[i, 3])) * d[1]
        out[i] = odd + even
        out[4 - i] = odd - even
    out[2] = (0.5 * (m[2, 0] - m[2, 4])) * d[0] + (0.5 * (m[2, 1] - m[2, 3])) * d[1]
    return out


def radial(f, coefs):
    total = coefs[0] * f[0:1, :]
    for k in range(1, 5):
        total = total + coefs[k] * f[k : k + 1, :]
    return total


def tile(j):
    return slice(NE * j, NE * j + NE)


def wide(ref):
    return jnp.concatenate([ref[j] for j in range(ref.shape[0])], axis=1)


def split(x):
    hi = x.astype(BF16)
    return hi, (x - hi.astype(F32)).astype(BF16)


def dot(a, b):
    return jnp.dot(a, b, preferred_element_type=F32)


def relane(x, matrix):
    return dot(jnp.concatenate(split(x), axis=1), matrix)


def split_tiles(x):
    lane = lax.broadcasted_iota(jnp.int32, (8, 128), 1)
    out = []
    for j in range(5):
        element = ((lane - j) * 77) & 127
        source = (5 * element + j) >> 7
        merged = x[0]
        for t in range(1, 5):
            merged = jnp.where(source == t, x[t], merged)
        out.append(jnp.take_along_axis(merged, (5 * lane + j) & 127, axis=1, mode="promise_in_bounds"))
    return out


def les_prims(q):
    rec = 1.0 / q[0]
    v = [q[1] * rec, q[2] * rec, q[3] * rec]
    p = 0.4 * (q[4] - 0.5 * (q[1] * v[0] + q[2] * v[1] + q[3] * v[2]))
    return rec, v, p


def les_flux(q, v, p, k):
    out = [q[1 + k]]
    for j in range(3):
        out.append(q[1 + j] * v[k] + p if j == k else q[1 + j] * v[k])
    out.append((q[4] + p) * v[k])
    return out


def les_speed(rec, v, p, k):
    return jnp.abs(v[k]) + jnp.sqrt(GAMMA * p * rec)


def common(fl, fr, sl, sr, ql, qr):
    half = 0.5 * jnp.maximum(sl, sr)
    return [0.5 * (fl[n] + fr[n]) - half * (qr[n] - ql[n]) for n in range(len(fl))]


def ape_carried(s):
    return s[6] * s[1] + s[7] * s[2] + s[8] * s[3] + s[0] / s[4]


def ape_leading(s, k):
    return s[5] * s[5] * s[4] * s[1 + k] + s[6 + k] * s[0]


def ape_common(l, r, k, fl=None, fr=None):
    if fl is None:
        fl = (ape_leading(l, k), ape_carried(l))
    if fr is None:
        fr = (ape_leading(r, k), ape_carried(r))
    half = 0.5 * jnp.maximum(jnp.abs(l[6 + k]) + l[5], jnp.abs(r[6 + k]) + r[5])
    out = []
    for n in range(4):
        value = -half * (r[n] - l[n])
        if n == 0:
            value = value + 0.5 * (fl[0] + fr[0])
        elif n == 1 + k:
            value = value + 0.5 * (fl[1] + fr[1])
        out.append(value)
    return out, fl, fr


B_ROWS, F_ROWS, G_ROWS = 224, 96, 160
B_APE = 176
F_APE = 50


def pack_kernel(
    les_h, ac_h, den_h, snd_h, mv_h, back, fwd, inner, outer, axial, les, ac, den, snd, mv, sems,
):
    halves = [slice(0, 5), slice(5, 10)]
    copies = [[], [], []]
    for h in range(2):
        for c in range(5):
            copies[h].append(pltpu.make_async_copy(les_h.at[c, halves[h]], les.at[c, halves[h]], sems.at[5 * h + c]))
    for i, (src, dst) in enumerate(((ac_h, ac), (den_h, den), (snd_h, snd), (mv_h, mv))):
        copies[2].append(pltpu.make_async_copy(src, dst, sems.at[10 + i]))
    for group in (0, 2, 1):
        for copy in copies[group]:
            copy.start()
    even = lax.rem(lax.axis_index("rad"), 2) == 0

    def radial_faces(layers):
        for j in range(5):
            for c in range(5):
                for a in layers:
                    first, last = les[c, a, 0:1, tile(j)], les[c, a, 9:10, tile(j)]
                    inner[j, c * 10 + a : c * 10 + a + 1, :] = jnp.where(even, last, first)
                    outer[j, c * 10 + a : c * 10 + a + 1, :] = jnp.where(even, first, last)

    for copy in copies[0]:
        copy.wait()
    for a in range(5):
        rec = 1.0 / les[0, a]
        for c in range(3):
            v = les[1 + c, a] * rec
            for j in range(5):
                back[j, c * 50 + a * 10 : c * 50 + a * 10 + 10, :] = v[:, tile(j)]
    for j in range(5):
        back[j, 150:160, :] = les[0, 0, :, tile(j)]
        back[j, 160:170, :] = les[4, 0, :, tile(j)]
        back[j, 170:176, :] = jnp.zeros((6, 128), F32)
        back[j, 221:224, :] = jnp.zeros((3, 128), F32)
        for buf in (fwd, inner, outer):
            buf[j, 95:96, :] = jnp.zeros((1, 128), F32)
    radial_faces(range(5))
    for copy in copies[2]:
        copy.wait()
    for j in range(5):
        for buf, a, base in ((back, 0, B_APE), (fwd, 4, F_APE)):
            for r in range(5):
                buf[j, pl.ds(base + r, 4, stride=5), :] = ac[a, r, :, tile(j)]
                buf[j, pl.ds(base + 30 + r, 3, stride=5), :] = mv[a, r, :, tile(j)]
            buf[j, base + 20 : base + 25, :] = den[a, :, tile(j)]
            buf[j, base + 25 : base + 30, :] = snd[a, :, tile(j)]
        for a in range(5):
            for src, base in ((ac, F_APE), (mv, F_APE + 30)):
                first, last = src[a, 0, :, tile(j)], src[a, 4, :, tile(j)]
                at = pl.ds(base + a, first.shape[0], stride=5)
                inner[j, at, :] = jnp.where(even, last, first)
                outer[j, at, :] = jnp.where(even, first, last)
            for src, base in ((den, F_APE + 20), (snd, F_APE + 25)):
                first, last = src[a, 0:1, tile(j)], src[a, 4:5, tile(j)]
                inner[j, base + a : base + a + 1, :] = jnp.where(even, last, first)
                outer[j, base + a : base + a + 1, :] = jnp.where(even, first, last)
    for copy in copies[1]:
        copy.wait()
    for j in range(5):
        for c in range(5):
            fwd[j, c * 10 : c * 10 + 10, :] = les[c, 9, :, tile(j)]
    radial_faces(range(5, 10))
    first = lax.axis_index("group") == 0

    def end(ref, *at):
        return jnp.where(first, ref[(*at, slice(None), slice(NX - 1, NX))], ref[(*at, slice(None), slice(0, 1))])

    def gather(columns, rows):
        lane = lax.broadcasted_iota(jnp.int32, (rows, 128), 1)
        value = jnp.broadcast_to(columns[0], (rows, 128))
        for i in range(1, len(columns)):
            value = jnp.where(lane == i, jnp.broadcast_to(columns[i], (rows, 128)), value)
        return value

    for c in range(5):
        axial[16 * c : 16 * c + 10, :] = gather([end(les, c, a) for a in range(10)], 10)
        axial[16 * c + 10 : 16 * c + 16, :] = jnp.ones((6, 128), F32)
    axial[80:84, :] = gather([end(ac, a, r) for a in range(5) for r in range(5)], 4)
    axial[84:87, :] = gather([end(mv, a, r) for a in range(5) for r in range(5)], 3)
    axial[87:88, :] = jnp.zeros((1, 128), F32)
    axial[88:93, :] = gather([end(den, a) for a in range(5)], 5)
    axial[93:96, :] = jnp.zeros((3, 128), F32)
    axial[96:101, :] = gather([end(snd, a) for a in range(5)], 5)
    axial[101:160, :] = jnp.zeros((59, 128), F32)


ROWS = 768
APE, APE_MV, APE_DEN, APE_SND = 504, 608, 688, 728


def interior_kernel(
    les, ac, den, snd, mv, proj, counts, elem, pattern, perm, coef,
    acc, da, lamb_out, m_out, pp,
    x, y, vel, omega, rt, one_hot, owned, flat,
):
    def list_matrices():
        upper = lax.broadcasted_iota(jnp.int32, (NE, NE), 1)
        lower = lax.broadcasted_iota(jnp.int32, (NE, NE), 0)
        row = jnp.broadcast_to(counts[...], (NE, NE)).astype(F32)
        ends = jnp.sum(jnp.where(upper <= lower, row, 0.0), axis=1, keepdims=True)
        starts = jnp.sum(jnp.where(upper < lower, row, 0.0), axis=1, keepdims=True)
        position = lax.broadcasted_iota(jnp.int32, (NE, 768), 1).astype(F32)
        mine = jnp.where((position >= starts) & (position < ends), jnp.broadcast_to(pattern[...], (NE, 768)), -1)
        for p in range(8):
            owned[p * NE : p * NE + NE, :] = jnp.where(mine == p, 1.0, 0.0).astype(BF16)
        source = jnp.broadcast_to(elem[...], (NE, 768))
        for i in range(6):
            which = lax.broadcasted_iota(jnp.int32, (NE, 768), 0) + i * NE
            one_hot[i * NE : i * NE + NE, :] = jnp.where(which == source, 1.0, 0.0).astype(BF16)
        m_out[...] = lax.dot_general(
            one_hot[...], owned[...], (((1,), (1,)), ((), ())), preferred_element_type=F32
        ).astype(BF16)

    def projection_matrices():
        flat[...] = jnp.zeros((1024, 128), F32)
        flat[0:1000, 0:125] = proj[...]
        for p in range(8):
            hi, lo = split(flat[pl.ds(p, 128, stride=8), :])
            pp[:, tile(p)] = hi
            pp[:, tile(8 + p)] = lo
            pp[:, tile(16 + p)] = hi

    def lane_splitting():
        for j in range(5):
            for c in range(5):
                for a in range(10):
                    x[j, c * 100 + a * 10 : c * 100 + a * 10 + 10, :] = les[c, a, :, tile(j)]
            for a in range(5):
                for r in range(5):
                    i = a * 5 + r
                    x[j, APE + 4 * i : APE + 4 * i + 4, :] = ac[a, r, :, tile(j)]
                    x[j, APE_MV + 3 * i : APE_MV + 3 * i + 3, :] = mv[a, r, :, tile(j)]
                x[j, APE_DEN + 8 * a : APE_DEN + 8 * a + 5, :] = den[a, :, tile(j)]
                x[j, APE_SND + 8 * a : APE_SND + 8 * a + 5, :] = snd[a, :, tile(j)]
        value = relane(jnp.concatenate([x[j, 0:512, :] for j in range(5)], axis=1), perm[...])
        for j in range(5):
            y[j, 0:504, :] = value[0:504, tile(j)]
        for i in range(63, 96):
            for j, part in enumerate(split_tiles([x[j, 8 * i : 8 * i + 8, :] for j in range(5)])):
                y[j, 8 * i : 8 * i + 8, :] = part

    def les_rows_pass():
        lane = lax.broadcasted_iota(jnp.int32, (8, 128), 1)

        @pl.loop(0, 20, unroll=5)
        def _(t):
            er = t // 10
            base = (t - er * 10) * 10 + er * 5
            rows = pl.ds(pl.multiple_of(t * 8, 8), 8)
            q = [[y[j, pl.ds(c * 100 + base, 8), :] for j in range(5)] for c in range(5)]
            rec, v, p = [], [[], [], []], []
            for j in range(5):
                rec_j, v_j, p_j = les_prims([q[c][j] for c in range(5)])
                rec.append(rec_j)
                p.append(p_j)
                for k in range(3):
                    v[k].append(v_j[k])
                    vel[k, j, rows, :] = v_j[k]
                vel[3, j, rows, :] = p_j
            coefs = [coef[er, k] for k in range(5)]
            flux = [les_flux([q[c][j] for c in range(5)], [v[k][j] for k in range(3)], p[j], 2) for j in range(5)]
            s_left = les_speed(rec[4], [v[k][4] for k in range(3)], p[4], 2)
            s_right = pltpu.roll(les_speed(rec[0], [v[k][0] for k in range(3)], p[0], 2), 127, 1)
            half = 0.5 * jnp.maximum(s_left, s_right)
            for n in range(5):
                fr = pltpu.roll(flux[0][n], 127, 1)
                qr = pltpu.roll(q[n][0], 127, 1)
                h = 0.5 * (flux[4][n] + fr) - half * (qr - q[n][4])
                out = apply5([flux[j][n] for j in range(5)], T)
                out[4] = out[4] - LIFT * jnp.where(lane < 127, h, flux[4][n])
                out[0] = out[0] + LIFT * jnp.where(lane > 0, pltpu.roll(h, 1, 1), flux[0][n])
                for j in range(5):
                    f = les_flux([q[c][j] for c in range(5)], [v[k][j] for k in range(3)], p[j], 1)[n]
                    acc[j, pl.ds(n * 100 + base, 5), :] = (out[j] + radial(f, coefs))[0:5]
            dcoefs = [coef[2, k] for k in range(5)]
            d2v0 = apply5(v[0], D)
            d2v1 = apply5(v[1], D)
            for j in range(5):
                omega[0, j, rows, :] = radial(v[2][j], dcoefs) - d2v1[j]
                omega[1, j, rows, :] = d2v0[j]
                omega[2, j, rows, :] = -radial(v[0][j], dcoefs)

    def les_azimuth_pass():
        for c in range(3):
            for i in range(4):
                rt[i, c * 128 + 120 : c * 128 + 128, :] = jnp.zeros((8, 128), F32)

        @pl.loop(0, 2)
        def _(er):
            for j in range(5):
                at = [pl.ds(pl.multiple_of(er * 80 + a * 8, 8), 8) for a in range(10)]
                q = [[y[j, pl.ds(c * 100 + a * 10 + er * 5, 8), :] for a in range(10)] for c in range(5)]
                v = [[vel[k, j, at[a], :] for a in range(10)] for k in range(3)]
                p = [vel[3, j, at[a], :] for a in range(10)]
                flux = [les_flux([q[c][a] for c in range(5)], [v[k][a] for k in range(3)], p[a], 0) for a in range(10)]
                speed = [jnp.abs(v[0][a]) + jnp.sqrt(GAMMA * p[a] / q[0][a]) for a in (4, 5)]
                h = common(flux[4], flux[5], speed[0], speed[1], [q[c][4] for c in range(5)], [q[c][5] for c in range(5)])
                for n in range(5):
                    low = apply5([flux[a][n] for a in range(5)], T)
                    low[0] = low[0] + LIFT * flux[0][n]
                    low[4] = low[4] - LIFT * h[n]
                    top = apply5([flux[5 + a][n] for a in range(5)], T)
                    top[0] = top[0] + LIFT * h[n]
                    top[4] = top[4] - LIFT * flux[9][n]
                    for a, value in enumerate(low + top):
                        to = pl.ds(n * 100 + a * 10 + er * 5, 5)
                        acc[j, to, :] = acc[j, to, :] + value[0:5]
                for ea in range(2):
                    d0v1 = apply5([v[1][5 * ea + i] for i in range(5)], D)
                    d0v2 = apply5([v[2][5 * ea + i] for i in range(5)], D)
                    for i in range(5):
                        a = 5 * ea + i
                        w0 = omega[0, j, at[a], :]
                        w1 = omega[1, j, at[a], :] - d0v2[i]
                        w2 = omega[2, j, at[a], :] + d0v1[i]
                        lamb = [
                            w1 * v[2][a] - w2 * v[1][a],
                            w2 * v[0][a] - w0 * v[2][a],
                            w0 * v[1][a] - w1 * v[0][a],
                        ]
                        for c in range(3):
                            rt[2 * ea + er, pl.ds(c * 128 + i * 25 + j, 5, stride=5), :] = lamb[c][0:5]
        for i in range(4):
            hi, lo = split(rt[i])
            lamb_out[0:384, tile(i)] = hi
            lamb_out[384:768, tile(i)] = lo

    def les_radial_face():
        for j in range(5):
            left = [pl.ds(c * 100 + 4, 10, stride=10) for c in range(5)]
            right = [pl.ds(c * 100 + 5, 10, stride=10) for c in range(5)]
            h, _, _ = les_common([y[j, at, :] for at in left], [y[j, at, :] for at in right], 1)
            for n in range(5):
                acc[j, left[n], :] = acc[j, left[n], :] - LIFT * h[n]
                acc[j, right[n], :] = acc[j, right[n], :] + LIFT * h[n]
            acc[j, 500:512, :] = jnp.zeros((12, 128), F32)

    def acoustic():
        lane5 = lax.broadcasted_iota(jnp.int32, (5, 128), 1)
        state = [[None] * 5 for _ in range(5)]
        for a in range(5):
            for j in range(5):
                state[a][j] = (
                    [y[j, pl.ds(APE + a * 20 + c, 5, stride=4), :] for c in range(4)]
                    + [y[j, base + a * 8 : base + a * 8 + 5, :] for base in (APE_DEN, APE_SND)]
                    + [y[j, pl.ds(APE_MV + a * 15 + k, 5, stride=3), :] for k in range(3)]
                )
        carried = [[ape_carried(state[a][j]) for j in range(5)] for a in range(5)]
        lead = [[[ape_leading(state[a][j], k) for j in range(5)] for a in range(5)] for k in range(3)]
        total = [[[None] * 5 for _ in range(5)] for _ in range(4)]
        minus = -D
        mcoefs = [coef[3, k, 0:5] for k in range(5)]
        for j in range(5):
            first = apply5([lead[0][a][j] for a in range(5)], minus)
            other = apply5([carried[a][j] for a in range(5)], minus)
            for a in range(5):
                total[0][a][j] = first[a] + radial(lead[1][a][j], mcoefs)
                total[1][a][j] = other[a]
                total[2][a][j] = radial(carried[a][j], mcoefs)
        for a in range(5):
            first = apply5(lead[2][a], T)
            other = apply5(carried[a], T)
            shift = [pltpu.roll(jnp.pad(v, ((0, 3), (0, 0))), 127, 1)[0:5] for v in state[a][0]]
            h, fl, fr = ape_common(state[a][4], shift, 2)
            for n in range(4):
                own4 = lead[2][a][4] if n == 0 else carried[a][4] if n == 3 else jnp.zeros_like(carried[a][4])
                own0 = lead[2][a][0] if n == 0 else carried[a][0] if n == 3 else jnp.zeros_like(carried[a][0])
                back = pltpu.roll(jnp.pad(h[n], ((0, 3), (0, 0))), 1, 1)[0:5]
                lift4 = -LIFT * jnp.where(lane5 < 127, h[n], own4)
                lift0 = LIFT * jnp.where(lane5 > 0, back, own0)
                for j in range(5):
                    value = total[n][a][j]
                    if n in (0, 3):
                        extra = first[j] if n == 0 else other[j]
                        value = extra if value is None else value + extra
                    if j == 4:
                        value = value + lift4
                    if j == 0:
                        value = value + lift0
                    if value is None:
                        value = jnp.zeros((5, 128), F32)
                    da[j, pl.ds(a * 20 + n, 5, stride=4), :] = value
        for j in range(5):
            da[j, 100:104, :] = jnp.zeros((4, 128), F32)

    for part in (
        list_matrices, projection_matrices, lane_splitting, les_rows_pass, les_azimuth_pass, les_radial_face, acoustic,
    ):
        part()


def ape_face(buf, base, j):
    return [buf[j, base + 5 * n : base + 5 * n + 5, :] for n in range(9)]


def back_face(buf, j):
    rho = buf[j, 150:160, :]
    return [rho] + [rho * buf[j, c * 50 : c * 50 + 10, :] for c in range(3)] + [buf[j, 160:170, :]]


def les_rows(buf, j):
    return [buf[j, c * 10 : c * 10 + 10, :] for c in range(5)]


def les_common(ql, qr, k):
    rl, vl, pl_ = les_prims(ql)
    rr, vr, pr = les_prims(qr)
    fl, fr = les_flux(ql, vl, pl_, k), les_flux(qr, vr, pr, k)
    return common(fl, fr, les_speed(rl, vl, pl_, k), les_speed(rr, vr, pr, k), ql, qr), fl, fr


def les_change(own, nbr, k, side):
    ro, vo, po = les_prims(own)
    rn, vn, pn = les_prims(nbr)
    fo, fn = les_flux(own, vo, po, k), les_flux(nbr, vn, pn, k)
    half = 0.5 * LIFT * jnp.maximum(les_speed(ro, vo, po, k), les_speed(rn, vn, pn, k))
    return [(0.5 * LIFT * side) * (fo[n] - fn[n]) + half * (nbr[n] - own[n]) for n in range(5)]


def ape_change(own, nbr, k, side):
    half = 0.5 * LIFT * jnp.maximum(jnp.abs(own[6 + k]) + own[5], jnp.abs(nbr[6 + k]) + nbr[5])
    out = [half * (nbr[n] - own[n]) for n in range(4)]
    out[0] = out[0] + (0.5 * LIFT * side) * (ape_leading(own, k) - ape_leading(nbr, k))
    out[1 + k] = out[1 + k] + (0.5 * LIFT * side) * (ape_carried(own) - ape_carried(nbr))
    return out


def finish_kernel(
    les, ac, acc, da_in, lamb_own, m, pp, back, fwd, inner, outer, axial,
    fwd_in, inner_in, outer_in, axial_in, back_in, perm, perm_t, coef,
    les_out, ac_out, delta, result, yn, rt, rhs, osc, da, sem,
):
    rad = lax.axis_index("rad")
    even = lax.rem(rad, 2) == 0
    first_half = lax.axis_index("group") == 0
    inner_side, axis_side = jnp.where(even, 1.0, -1.0), jnp.where(first_half, 1.0, -1.0)
    inner_row = jnp.where(even, 9, 0)
    at_end = (rad == 0) | (rad == lax.axis_size("rad") - 1)

    def les_faces():
        value = relane(wide(acc), perm_t[...])
        for j in range(5):
            delta[j] = value[:, tile(j)]
        for j in range(5):

            def add(start, stride, change):
                for n in range(5):
                    at = pl.ds(n * 100 + start, 10, stride=stride)
                    delta[j, at, :] = delta[j, at, :] + change[n]

            add(inner_row, 10, les_change(les_rows(inner, j), les_rows(inner_in, j), 1, inner_side))
            own = les_rows(outer, j)
            nbr = [jnp.where(at_end, o, n) for o, n in zip(own, les_rows(outer_in, j))]
            add(9 - inner_row, 10, les_change(own, nbr, 1, -inner_side))
            add(0, 1, les_change(back_face(back, j), les_rows(fwd_in, j), 0, -1.0))
            add(90, 1, les_change(les_rows(fwd, j), back_face(back_in, j), 0, 1.0))
        own = [axial[16 * c : 16 * c + 16, :] for c in range(5)]
        nbr = [axial_in[16 * c : 16 * c + 16, :] for c in range(5)]
        change = les_change(own, nbr, 2, axis_side)
        lane = lax.broadcasted_iota(jnp.int32, (10, 128), 1)
        on_last = (lane == 127) & first_half
        on_first = (lane == 0) & jnp.logical_not(first_half)
        for n in range(5):
            for a in range(10):
                column = jnp.broadcast_to(change[n][0:10, a : a + 1], (10, 128))
                at = slice(n * 100 + a * 10, n * 100 + a * 10 + 10)
                for j in range(5):
                    value = delta[j, at, :]
                    if j == 0:
                        value = value + jnp.where(on_first, column, 0.0)
                    if j == 4:
                        value = value + jnp.where(on_last, column, 0.0)
                    result[n, a, :, tile(j)] = les[n, a, :, tile(j)] + DT * value

    def send_les():
        pltpu.make_async_copy(result, les_out, sem).start()

    def sources():
        value = relane(jnp.concatenate([back_in[j, 0:160, :] for j in range(5)], axis=1), perm[...])
        for j in range(5):
            yn[j] = value[:, tile(j)]
        for c in range(3):
            for i in range(2):
                rt[i, c * 128 + 120 : c * 128 + 128, :] = jnp.zeros((8, 128), F32)
        dcoefs = [coef[2, k] for k in range(5)]
        for er in range(2):
            v = [[[None] * 5 for _ in range(5)] for _ in range(3)]
            for c in range(3):
                for a in range(5):
                    at = c * 50 + a * 10 + er * 5
                    v[c][a] = [yn[j, at : at + 8, :] for j in range(5)]
            d2v0 = [apply5(v[0][a], D) for a in range(5)]
            d2v1 = [apply5(v[1][a], D) for a in range(5)]
            for j in range(5):
                d0v1 = apply5([v[1][a][j] for a in range(5)], D)
                d0v2 = apply5([v[2][a][j] for a in range(5)], D)
                for a in range(5):
                    w0 = radial(v[2][a][j], dcoefs) - d2v1[a][j]
                    w1 = d2v0[a][j] - d0v2[a]
                    w2 = d0v1[a] - radial(v[0][a][j], dcoefs)
                    lamb = [
                        w1 * v[2][a][j] - w2 * v[1][a][j],
                        w2 * v[0][a][j] - w0 * v[2][a][j],
                        w0 * v[1][a][j] - w1 * v[0][a][j],
                    ]
                    for c in range(3):
                        rt[er, pl.ds(c * 128 + a * 25 + j, 5, stride=5), :] = lamb[c][0:5]
        near = jnp.concatenate(split(wide(rt)), axis=0)
        s = dot(jnp.concatenate([lamb_own[...], near], axis=1), m[...])
        s = s[0:384] + s[384:768]
        for p in range(8):
            for c in range(3):
                hi, lo = split(s[c * 128 : c * 128 + 128, tile(p)])
                rhs[p * 128 : p * 128 + 128, tile(c)] = hi
                rhs[1024 + p * 128 : 1152 + p * 128, tile(c)] = hi
                rhs[2048 + p * 128 : 2176 + p * 128, tile(c)] = lo
        out = dot(pp[...], rhs[...])
        for c in range(3):
            osc[c] = out[:, tile(c)]

    def acoustic():
        for j in range(5):
            da[j] = da_in[j]
            for a in range(5):
                for n in range(1, 4):
                    at = pl.ds(a * 20 + n, 5, stride=4)
                    da[j, at, :] = da[j, at, :] - osc[n - 1, pl.ds(a * 25 + j, 5, stride=5), :]
        value = relane(wide(da), perm_t[...])

        def axial_state(buf):
            def spread(base):
                rows = buf[base : base + 8, :]
                row = lax.broadcasted_iota(jnp.int32, (8, 128), 0)
                lanes = lax.broadcasted_iota(jnp.int32, (8, 128), 1)
                out = jnp.zeros((8, 128), F32)
                for a in range(5):
                    here = (lanes == a * 5 + row) & (row < 5)
                    out = jnp.where(here, jnp.broadcast_to(rows[:, a : a + 1], (8, 128)), out)
                return jnp.sum(out, axis=0, keepdims=True)

            used = lax.broadcasted_iota(jnp.int32, (1, 128), 1) < 25
            return (
                [buf[80 + c : 81 + c, :] for c in range(4)]
                + [jnp.where(used, spread(88), 1.0), spread(96)]
                + [buf[84 + k : 85 + k, :] for k in range(3)]
            )

        own, nbr = axial_state(axial), axial_state(axial_in)
        axis = jnp.concatenate(ape_change(own, nbr, 2, axis_side), axis=0)
        lane4 = lax.broadcasted_iota(jnp.int32, (4, 128), 1)
        on_last = (lane4 == 127) & first_half
        on_first = (lane4 == 0) & jnp.logical_not(first_half)
        for j in range(5):
            da[j] = value[:, tile(j)]

            def add(start, stride, change):
                for n in range(4):
                    at = pl.ds(start + n, 5, stride=stride)
                    da[j, at, :] = da[j, at, :] + change[n]

            add(0, 4, ape_change(ape_face(back, B_APE, j), ape_face(fwd_in, F_APE, j), 0, -1.0))
            add(80, 4, ape_change(ape_face(fwd, F_APE, j), ape_face(back_in, B_APE, j), 0, 1.0))
            own, nbr = ape_face(inner, F_APE, j), ape_face(inner_in, F_APE, j)
            add(jnp.where(even, 16, 0), 20, ape_change(own, nbr, 1, inner_side))
            own = ape_face(outer, F_APE, j)
            nbr = [jnp.where(at_end, o, n) for o, n in zip(own, ape_face(outer_in, F_APE, j))]
            add(jnp.where(even, 0, 16), 20, ape_change(own, nbr, 1, -inner_side))
            for a in range(5):
                for r in range(5):
                    i = a * 5 + r
                    change = da[j, 4 * i : 4 * i + 4, :]
                    if j == 0 or j == 4:
                        column = jnp.broadcast_to(axis[:, i : i + 1], (4, 128))
                        change = change + jnp.where(on_last if j == 4 else on_first, column, 0.0)
                    ac_out[a, r, :, tile(j)] = ac[a, r, :, tile(j)] + DT * change

    for part in (les_faces, send_les, sources, acoustic):
        part()
    pltpu.make_async_copy(result, les_out, sem).wait()


def shape(*dims, dtype=F32):
    return jax.ShapeDtypeStruct(dims, dtype)


def cost(flops, size):
    return pl.CostEstimate(flops=flops, bytes_accessed=size, transcendentals=0)


def params():
    return pltpu.CompilerParams(vmem_limit_bytes=VMEM_LIMIT)


def body(les, ac, den, snd, mv, proj, counts, elem, pattern):
    vmem = pl.BlockSpec(memory_space=pltpu.VMEM)
    ac = jnp.transpose(ac, (1, 2, 0, 3))
    mv = jnp.transpose(mv, (1, 2, 0, 3))
    proj = jnp.transpose(proj, (1, 0, 2)).reshape(1000, 125)
    counts, elem, pattern = counts.reshape(1, 128), elem.reshape(1, 768), pattern.reshape(1, 768)
    perm = jnp.asarray(np.tile(lane_split(), (2, 1)), BF16)
    perm_t = jnp.asarray(np.tile(lane_split().T, (2, 1)), BF16)
    coef = jnp.asarray(radial_coefs(), F32)

    hbm = pl.BlockSpec(memory_space=pltpu.HBM)
    held = [pltpu.VMEM(a.shape, F32) for a in (les, ac, den, snd, mv)]
    back, fwd, inner, outer, axial, les, ac, den, snd, mv = pl.pallas_call(
        pack_kernel,
        out_shape=[pltpu.VMEM((5, n, 128), F32) for n in (B_ROWS, F_ROWS, F_ROWS, F_ROWS)]
        + [pltpu.VMEM((G_ROWS, 128), F32)]
        + held,
        in_specs=[hbm] * 5,
        out_specs=[vmem] * 10,
        scratch_shapes=[pltpu.SemaphoreType.DMA((14,))],
        compiler_params=params(),
        cost_estimate=cost(1_000_000, 5_000_000),
        name="pack",
    )(*[pltpu.with_memory_space_constraint(a, pltpu.HBM) for a in (les, ac, den, snd, mv)])

    azim, radc = lax.axis_size("azim"), lax.axis_size("rad")
    back_in = lax.ppermute(back, "azim", [(i, (i - 1) % azim) for i in range(azim)])
    fwd_in = lax.ppermute(fwd, "azim", [(i, (i + 1) % azim) for i in range(azim)])
    inner_in = lax.ppermute(inner, "rad", [(i, i ^ 1) for i in range(radc)])
    outer_in = lax.ppermute(outer, "rad", [p for i in range(1, radc - 1, 2) for p in ((i, i + 1), (i + 1, i))])
    axial_in = lax.ppermute(axial, "group", [(0, 1), (1, 0)])

    acc, da, lamb, m, pp = pl.pallas_call(
        interior_kernel,
        out_shape=[
            shape(5, 512, 128), shape(5, 104, 128), shape(768, 512, dtype=BF16), shape(768, 1024, dtype=BF16),
            shape(128, 3072, dtype=BF16),
        ],
        in_specs=[vmem] * 11,
        out_specs=[vmem] * 5,
        scratch_shapes=[
            pltpu.VMEM((5, ROWS, 128), F32),
            pltpu.VMEM((5, ROWS, 128), F32),
            pltpu.VMEM((4, 5, 160, 128), F32),
            pltpu.VMEM((3, 5, 160, 128), F32),
            pltpu.VMEM((4, 384, 128), F32),
            pltpu.VMEM((768, 768), BF16),
            pltpu.VMEM((1024, 768), BF16),
            pltpu.VMEM((1024, 128), F32),
        ],
        compiler_params=params(),
        cost_estimate=cost(5_000_000_000, 10_000_000),
        name="interior",
    )(les, ac, den, snd, mv, proj, counts, elem, pattern, perm, coef)

    les_next, ac_next = pl.pallas_call(
        finish_kernel,
        out_shape=[shape(5, 10, 10, NX), shape(5, 5, 4, NX)],
        in_specs=[vmem] * 20,
        out_specs=[hbm, vmem],
        scratch_shapes=[
            pltpu.VMEM((5, 512, 128), F32),
            pltpu.VMEM((5, 10, 10, NX), F32),
            pltpu.VMEM((5, 160, 128), F32),
            pltpu.VMEM((2, 384, 128), F32),
            pltpu.VMEM((3072, 384), BF16),
            pltpu.VMEM((3, 128, 128), F32),
            pltpu.VMEM((5, 104, 128), F32),
            pltpu.SemaphoreType.DMA(()),
        ],
        compiler_params=params(),
        cost_estimate=cost(500_000_000, 4_000_000),
        name="finish",
    )(
        les, ac, acc, da, lamb, m, pp, back, fwd, inner, outer, axial,
        fwd_in, inner_in, outer_in, axial_in, back_in, perm, perm_t, coef,
    )
    return les_next, jnp.transpose(ac_next, (2, 0, 1, 3))


def solution(mesh):
    field = P(None, "azim", "rad", "group")
    node = P("azim", "rad", "group")
    lists = P("azim", "rad", "group", None)
    return jax.shard_map(
        body,
        mesh=mesh,
        in_specs=(field, field, node, node, field, P(), lists, lists, lists),
        out_specs=(field, field),
        check_vma=False,
    )
```

```python
import functools
import math

import jax
import jax.numpy as jnp
import numpy as np
from jax import lax
from jax.experimental import pallas as pl
from jax.experimental.pallas import tpu as pltpu
from jax.sharding import PartitionSpec as P

GAMMA = 1.4
DT = 0.05
LIFT = 10.0
F32 = jnp.float32
BF16 = jnp.bfloat16
NX = 640
NE = 128
VMEM_LIMIT = 40 * 1024 * 1024


def derivative_matrix():
    points = np.array([-1.0, -math.sqrt(3.0 / 7.0), 0.0, math.sqrt(3.0 / 7.0), 1.0])
    weights = np.array([1.0 / np.prod([points[j] - points[k] for k in range(5) if k != j]) for j in range(5)])
    matrix = np.zeros((5, 5))
    for i in range(5):
        for j in range(5):
            if i != j:
                matrix[i, j] = weights[j] / weights[i] / (points[i] - points[j])
        matrix[i, i] = -np.sum(matrix[i])
    return matrix


D = derivative_matrix()
T = -D.copy()
T[0, 0] -= LIFT
T[4, 4] += LIFT


def lane_split():
    p = np.zeros((NX, NX), np.float32)
    for e in range(NE):
        for j in range(5):
            p[5 * e + j, NE * j + e] = 1.0
    return p


def radial_coefs():
    inner, outer = T.copy(), T.copy()
    inner[0, 0] += LIFT
    outer[4, 4] -= LIFT
    out = np.zeros((4, 5, 8, 128), np.float32)
    for kind, m in enumerate((inner, outer, D, -D)):
        for k in range(5):
            out[kind, k, :5, :] = m[:, k][:, None]
    return out


def apply5(f, m):
    s = [f[0] + f[4], f[1] + f[3]]
    d = [f[0] - f[4], f[1] - f[3]]
    out = [None] * 5
    for i in range(2):
        even = (0.5 * (m[i, 0] + m[i, 4])) * s[0] + (0.5 * (m[i, 1] + m[i, 3])) * s[1] + m[i, 2] * f[2]
        odd = (0.5 * (m[i, 0] - m[i, 4])) * d[0] + (0.5 * (m[i, 1] - m[i, 3])) * d[1]
        out[i] = odd + even
        out[4 - i] = odd - even
    out[2] = (0.5 * (m[2, 0] - m[2, 4])) * d[0] + (0.5 * (m[2, 1] - m[2, 3])) * d[1]
    return out


def radial(f, coefs):
    total = coefs[0] * f[0:1, :]
    for k in range(1, 5):
        total = total + coefs[k] * f[k : k + 1, :]
    return total


def tile(j):
    return slice(NE * j, NE * j + NE)


def wide(ref):
    return jnp.concatenate([ref[j] for j in range(ref.shape[0])], axis=1)


def split(x):
    hi = x.astype(BF16)
    return hi, (x - hi.astype(F32)).astype(BF16)


def dot(a, b):
    return jnp.dot(a, b, preferred_element_type=F32)


def relane(x, matrix):
    return dot(jnp.concatenate(split(x), axis=1), matrix)


def split_tiles(x):
    lane = lax.broadcasted_iota(jnp.int32, (8, 128), 1)
    out = []
    for j in range(5):
        element = ((lane - j) * 77) & 127
        source = (5 * element + j) >> 7
        merged = x[0]
        for t in range(1, 5):
            merged = jnp.where(source == t, x[t], merged)
        out.append(jnp.take_along_axis(merged, (5 * lane + j) & 127, axis=1, mode="promise_in_bounds"))
    return out


def les_prims(q):
    rec = 1.0 / q[0]
    v = [q[1] * rec, q[2] * rec, q[3] * rec]
    p = 0.4 * (q[4] - 0.5 * (q[1] * v[0] + q[2] * v[1] + q[3] * v[2]))
    return rec, v, p


def les_flux(q, v, p, k):
    out = [q[1 + k]]
    for j in range(3):
        out.append(q[1 + j] * v[k] + p if j == k else q[1 + j] * v[k])
    out.append((q[4] + p) * v[k])
    return out


def les_speed(rec, v, p, k):
    return jnp.abs(v[k]) + jnp.sqrt(GAMMA * p * rec)


def common(fl, fr, sl, sr, ql, qr):
    half = 0.5 * jnp.maximum(sl, sr)
    return [0.5 * (fl[n] + fr[n]) - half * (qr[n] - ql[n]) for n in range(len(fl))]


def ape_carried(s):
    return s[6] * s[1] + s[7] * s[2] + s[8] * s[3] + s[0] / s[4]


def ape_leading(s, k):
    return s[5] * s[5] * s[4] * s[1 + k] + s[6 + k] * s[0]


def ape_common(l, r, k, fl=None, fr=None):
    if fl is None:
        fl = (ape_leading(l, k), ape_carried(l))
    if fr is None:
        fr = (ape_leading(r, k), ape_carried(r))
    half = 0.5 * jnp.maximum(jnp.abs(l[6 + k]) + l[5], jnp.abs(r[6 + k]) + r[5])
    out = []
    for n in range(4):
        value = -half * (r[n] - l[n])
        if n == 0:
            value = value + 0.5 * (fl[0] + fr[0])
        elif n == 1 + k:
            value = value + 0.5 * (fl[1] + fr[1])
        out.append(value)
    return out, fl, fr


B_ROWS, F_ROWS, G_ROWS = 224, 96, 160
B_APE = 176
F_APE = 50


def pack_kernel(
    les_h, ac_h, den_h, snd_h, mv_h, back, fwd, inner, outer, axial, les, ac, den, snd, mv, sems,
):
    halves = [slice(0, 5), slice(5, 10)]
    copies = [[], [], []]
    for h in range(2):
        for c in range(5):
            copies[h].append(pltpu.make_async_copy(les_h.at[c, halves[h]], les.at[c, halves[h]], sems.at[5 * h + c]))
    for i, (src, dst) in enumerate(((ac_h, ac), (den_h, den), (snd_h, snd), (mv_h, mv))):
        copies[2].append(pltpu.make_async_copy(src, dst, sems.at[10 + i]))
    for group in (0, 2, 1):
        for copy in copies[group]:
            copy.start()
    even = lax.rem(lax.axis_index("rad"), 2) == 0

    def radial_faces(layers):
        for j in range(5):
            for c in range(5):
                for a in layers:
                    first, last = les[c, a, 0:1, tile(j)], les[c, a, 9:10, tile(j)]
                    inner[j, c * 10 + a : c * 10 + a + 1, :] = jnp.where(even, last, first)
                    outer[j, c * 10 + a : c * 10 + a + 1, :] = jnp.where(even, first, last)

    for copy in copies[0]:
        copy.wait()
    for a in range(5):
        rec = 1.0 / les[0, a]
        for c in range(3):
            v = les[1 + c, a] * rec
            for j in range(5):
                back[j, c * 50 + a * 10 : c * 50 + a * 10 + 10, :] = v[:, tile(j)]
    for j in range(5):
        back[j, 150:160, :] = les[0, 0, :, tile(j)]
        back[j, 160:170, :] = les[4, 0, :, tile(j)]
        back[j, 170:176, :] = jnp.zeros((6, 128), F32)
        back[j, 221:224, :] = jnp.zeros((3, 128), F32)
        for buf in (fwd, inner, outer):
            buf[j, 95:96, :] = jnp.zeros((1, 128), F32)
    radial_faces(range(5))
    for copy in copies[2]:
        copy.wait()
    for j in range(5):
        for buf, a, base in ((back, 0, B_APE), (fwd, 4, F_APE)):
            for r in range(5):
                buf[j, pl.ds(base + r, 4, stride=5), :] = ac[a, r, :, tile(j)]
                buf[j, pl.ds(base + 30 + r, 3, stride=5), :] = mv[a, r, :, tile(j)]
            buf[j, base + 20 : base + 25, :] = den[a, :, tile(j)]
            buf[j, base + 25 : base + 30, :] = snd[a, :, tile(j)]
        for a in range(5):
            for src, base in ((ac, F_APE), (mv, F_APE + 30)):
                first, last = src[a, 0, :, tile(j)], src[a, 4, :, tile(j)]
                at = pl.ds(base + a, first.shape[0], stride=5)
                inner[j, at, :] = jnp.where(even, last, first)
                outer[j, at, :] = jnp.where(even, first, last)
            for src, base in ((den, F_APE + 20), (snd, F_APE + 25)):
                first, last = src[a, 0:1, tile(j)], src[a, 4:5, tile(j)]
                inner[j, base + a : base + a + 1, :] = jnp.where(even, last, first)
                outer[j, base + a : base + a + 1, :] = jnp.where(even, first, last)
    for copy in copies[1]:
        copy.wait()
    for j in range(5):
        for c in range(5):
            fwd[j, c * 10 : c * 10 + 10, :] = les[c, 9, :, tile(j)]
    radial_faces(range(5, 10))
    first = lax.axis_index("group") == 0

    def end(ref, *at):
        return jnp.where(first, ref[(*at, slice(None), slice(NX - 1, NX))], ref[(*at, slice(None), slice(0, 1))])

    def gather(columns, rows):
        lane = lax.broadcasted_iota(jnp.int32, (rows, 128), 1)
        value = jnp.broadcast_to(columns[0], (rows, 128))
        for i in range(1, len(columns)):
            value = jnp.where(lane == i, jnp.broadcast_to(columns[i], (rows, 128)), value)
        return value

    for c in range(5):
        axial[16 * c : 16 * c + 10, :] = gather([end(les, c, a) for a in range(10)], 10)
        axial[16 * c + 10 : 16 * c + 16, :] = jnp.ones((6, 128), F32)
    axial[80:84, :] = gather([end(ac, a, r) for a in range(5) for r in range(5)], 4)
    axial[84:87, :] = gather([end(mv, a, r) for a in range(5) for r in range(5)], 3)
    axial[87:88, :] = jnp.zeros((1, 128), F32)
    axial[88:93, :] = gather([end(den, a) for a in range(5)], 5)
    axial[93:96, :] = jnp.zeros((3, 128), F32)
    axial[96:101, :] = gather([end(snd, a) for a in range(5)], 5)
    axial[101:160, :] = jnp.zeros((59, 128), F32)


ROWS = 768
APE, APE_MV, APE_DEN, APE_SND = 504, 608, 688, 728


def interior_kernel(
    les, ac, den, snd, mv, proj, counts, elem, pattern, perm, coef,
    acc, da, lamb_out, m_out, pp,
    x, y, vel, omega, rt, one_hot, owned, flat,
):
    def list_matrices():
        upper = lax.broadcasted_iota(jnp.int32, (NE, NE), 1)
        lower = lax.broadcasted_iota(jnp.int32, (NE, NE), 0)
        row = jnp.broadcast_to(counts[...], (NE, NE)).astype(F32)
        ends = jnp.sum(jnp.where(upper <= lower, row, 0.0), axis=1, keepdims=True)
        starts = jnp.sum(jnp.where(upper < lower, row, 0.0), axis=1, keepdims=True)
        position = lax.broadcasted_iota(jnp.int32, (NE, 768), 1).astype(F32)
        mine = jnp.where((position >= starts) & (position < ends), jnp.broadcast_to(pattern[...], (NE, 768)), -1)
        for p in range(8):
            owned[p * NE : p * NE + NE, :] = jnp.where(mine == p, 1.0, 0.0).astype(BF16)
        source = jnp.broadcast_to(elem[...], (NE, 768))
        for i in range(6):
            which = lax.broadcasted_iota(jnp.int32, (NE, 768), 0) + i * NE
            one_hot[i * NE : i * NE + NE, :] = jnp.where(which == source, 1.0, 0.0).astype(BF16)
        m_out[...] = lax.dot_general(
            one_hot[...], owned[...], (((1,), (1,)), ((), ())), preferred_element_type=F32
        ).astype(BF16)

    def projection_matrices():
        flat[...] = jnp.zeros((1024, 128), F32)
        flat[0:1000, 0:125] = proj[...]
        for p in range(8):
            hi, lo = split(flat[pl.ds(p, 128, stride=8), :])
            pp[:, tile(p)] = hi
            pp[:, tile(8 + p)] = lo
            pp[:, tile(16 + p)] = hi

    def lane_splitting():
        for j in range(5):
            for c in range(5):
                for a in range(10):
                    x[j, c * 100 + a * 10 : c * 100 + a * 10 + 10, :] = les[c, a, :, tile(j)]
            for a in range(5):
                for r in range(5):
                    i = a * 5 + r
                    x[j, APE + 4 * i : APE + 4 * i + 4, :] = ac[a, r, :, tile(j)]
                    x[j, APE_MV + 3 * i : APE_MV + 3 * i + 3, :] = mv[a, r, :, tile(j)]
                x[j, APE_DEN + 8 * a : APE_DEN + 8 * a + 5, :] = den[a, :, tile(j)]
                x[j, APE_SND + 8 * a : APE_SND + 8 * a + 5, :] = snd[a, :, tile(j)]
        value = relane(jnp.concatenate([x[j, 0:512, :] for j in range(5)], axis=1), perm[...])
        for j in range(5):
            y[j, 0:504, :] = value[0:504, tile(j)]
        for i in range(63, 96):
            for j, part in enumerate(split_tiles([x[j, 8 * i : 8 * i + 8, :] for j in range(5)])):
                y[j, 8 * i : 8 * i + 8, :] = part

    def les_rows_pass():
        lane = lax.broadcasted_iota(jnp.int32, (8, 128), 1)

        @pl.loop(0, 20, unroll=5)
        def _(t):
            er = t // 10
            base = (t - er * 10) * 10 + er * 5
            rows = pl.ds(pl.multiple_of(t * 8, 8), 8)
            q = [[y[j, pl.ds(c * 100 + base, 8), :] for j in range(5)] for c in range(5)]
            rec, v, p = [], [[], [], []], []
            for j in range(5):
                rec_j, v_j, p_j = les_prims([q[c][j] for c in range(5)])
                rec.append(rec_j)
                p.append(p_j)
                for k in range(3):
                    v[k].append(v_j[k])
                    vel[k, j, rows, :] = v_j[k]
                vel[3, j, rows, :] = p_j
            coefs = [coef[er, k] for k in range(5)]
            flux = [les_flux([q[c][j] for c in range(5)], [v[k][j] for k in range(3)], p[j], 2) for j in range(5)]
            s_left = les_speed(rec[4], [v[k][4] for k in range(3)], p[4], 2)
            s_right = pltpu.roll(les_speed(rec[0], [v[k][0] for k in range(3)], p[0], 2), 127, 1)
            half = 0.5 * jnp.maximum(s_left, s_right)
            for n in range(5):
                fr = pltpu.roll(flux[0][n], 127, 1)
                qr = pltpu.roll(q[n][0], 127, 1)
                h = 0.5 * (flux[4][n] + fr) - half * (qr - q[n][4])
                out = apply5([flux[j][n] for j in range(5)], T)
                out[4] = out[4] - LIFT * jnp.where(lane < 127, h, flux[4][n])
                out[0] = out[0] + LIFT * jnp.where(lane > 0, pltpu.roll(h, 1, 1), flux[0][n])
                for j in range(5):
                    f = les_flux([q[c][j] for c in range(5)], [v[k][j] for k in range(3)], p[j], 1)[n]
                    acc[j, pl.ds(n * 100 + base, 5), :] = (out[j] + radial(f, coefs))[0:5]
            dcoefs = [coef[2, k] for k in range(5)]
            d2v0 = apply5(v[0], D)
            d2v1 = apply5(v[1], D)
            for j in range(5):
                omega[0, j, rows, :] = radial(v[2][j], dcoefs) - d2v1[j]
                omega[1, j, rows, :] = d2v0[j]
                omega[2, j, rows, :] = -radial(v[0][j], dcoefs)

    def les_azimuth_pass():
        for c in range(3):
            for i in range(4):
                rt[i, c * 128 + 120 : c * 128 + 128, :] = jnp.zeros((8, 128), F32)

        @pl.loop(0, 2)
        def _(er):
            for j in range(5):
                at = [pl.ds(pl.multiple_of(er * 80 + a * 8, 8), 8) for a in range(10)]
                q = [[y[j, pl.ds(c * 100 + a * 10 + er * 5, 8), :] for a in range(10)] for c in range(5)]
                v = [[vel[k, j, at[a], :] for a in range(10)] for k in range(3)]
                p = [vel[3, j, at[a], :] for a in range(10)]
                flux = [les_flux([q[c][a] for c in range(5)], [v[k][a] for k in range(3)], p[a], 0) for a in range(10)]
                speed = [jnp.abs(v[0][a]) + jnp.sqrt(GAMMA * p[a] / q[0][a]) for a in (4, 5)]
                h = common(flux[4], flux[5], speed[0], speed[1], [q[c][4] for c in range(5)], [q[c][5] for c in range(5)])
                for n in range(5):
                    low = apply5([flux[a][n] for a in range(5)], T)
                    low[0] = low[0] + LIFT * flux[0][n]
                    low[4] = low[4] - LIFT * h[n]
                    top = apply5([flux[5 + a][n] for a in range(5)], T)
                    top[0] = top[0] + LIFT * h[n]
                    top[4] = top[4] - LIFT * flux[9][n]
                    for a, value in enumerate(low + top):
                        to = pl.ds(n * 100 + a * 10 + er * 5, 5)
                        acc[j, to, :] = acc[j, to, :] + value[0:5]
                for ea in range(2):
                    d0v1 = apply5([v[1][5 * ea + i] for i in range(5)], D)
                    d0v2 = apply5([v[2][5 * ea + i] for i in range(5)], D)
                    for i in range(5):
                        a = 5 * ea + i
                        w0 = omega[0, j, at[a], :]
                        w1 = omega[1, j, at[a], :] - d0v2[i]
                        w2 = omega[2, j, at[a], :] + d0v1[i]
                        lamb = [
                            w1 * v[2][a] - w2 * v[1][a],
                            w2 * v[0][a] - w0 * v[2][a],
                            w0 * v[1][a] - w1 * v[0][a],
                        ]
                        for c in range(3):
                            rt[2 * ea + er, pl.ds(c * 128 + i * 25 + j, 5, stride=5), :] = lamb[c][0:5]
        for i in range(4):
            hi, lo = split(rt[i])
            lamb_out[0:384, tile(i)] = hi
            lamb_out[384:768, tile(i)] = lo

    def les_radial_face():
        for j in range(5):
            left = [pl.ds(c * 100 + 4, 10, stride=10) for c in range(5)]
            right = [pl.ds(c * 100 + 5, 10, stride=10) for c in range(5)]
            h, _, _ = les_common([y[j, at, :] for at in left], [y[j, at, :] for at in right], 1)
            for n in range(5):
                acc[j, left[n], :] = acc[j, left[n], :] - LIFT * h[n]
                acc[j, right[n], :] = acc[j, right[n], :] + LIFT * h[n]
            acc[j, 500:512, :] = jnp.zeros((12, 128), F32)

    def acoustic():
        lane5 = lax.broadcasted_iota(jnp.int32, (5, 128), 1)
        state = [[None] * 5 for _ in range(5)]
        for a in range(5):
            for j in range(5):
                state[a][j] = (
                    [y[j, pl.ds(APE + a * 20 + c, 5, stride=4), :] for c in range(4)]
                    + [y[j, base + a * 8 : base + a * 8 + 5, :] for base in (APE_DEN, APE_SND)]
                    + [y[j, pl.ds(APE_MV + a * 15 + k, 5, stride=3), :] for k in range(3)]
                )
        carried = [[ape_carried(state[a][j]) for j in range(5)] for a in range(5)]
        lead = [[[ape_leading(state[a][j], k) for j in range(5)] for a in range(5)] for k in range(3)]
        total = [[[None] * 5 for _ in range(5)] for _ in range(4)]
        minus = -D
        mcoefs = [coef[3, k, 0:5] for k in range(5)]
        for j in range(5):
            first = apply5([lead[0][a][j] for a in range(5)], minus)
            other = apply5([carried[a][j] for a in range(5)], minus)
            for a in range(5):
                total[0][a][j] = first[a] + radial(lead[1][a][j], mcoefs)
                total[1][a][j] = other[a]
                total[2][a][j] = radial(carried[a][j], mcoefs)
        for a in range(5):
            first = apply5(lead[2][a], T)
            other = apply5(carried[a], T)
            shift = [pltpu.roll(jnp.pad(v, ((0, 3), (0, 0))), 127, 1)[0:5] for v in state[a][0]]
            h, fl, fr = ape_common(state[a][4], shift, 2)
            for n in range(4):
                own4 = lead[2][a][4] if n == 0 else carried[a][4] if n == 3 else jnp.zeros_like(carried[a][4])
                own0 = lead[2][a][0] if n == 0 else carried[a][0] if n == 3 else jnp.zeros_like(carried[a][0])
                back = pltpu.roll(jnp.pad(h[n], ((0, 3), (0, 0))), 1, 1)[0:5]
                lift4 = -LIFT * jnp.where(lane5 < 127, h[n], own4)
                lift0 = LIFT * jnp.where(lane5 > 0, back, own0)
                for j in range(5):
                    value = total[n][a][j]
                    if n in (0, 3):
                        extra = first[j] if n == 0 else other[j]
                        value = extra if value is None else value + extra
                    if j == 4:
                        value = value + lift4
                    if j == 0:
                        value = value + lift0
                    if value is None:
                        value = jnp.zeros((5, 128), F32)
                    da[j, pl.ds(a * 20 + n, 5, stride=4), :] = value
        for j in range(5):
            da[j, 100:104, :] = jnp.zeros((4, 128), F32)

    for part in (
        list_matrices, projection_matrices, lane_splitting, les_rows_pass, les_azimuth_pass, les_radial_face, acoustic,
    ):
        part()


def ape_face(buf, base, j):
    return [buf[j, base + 5 * n : base + 5 * n + 5, :] for n in range(9)]


def back_face(buf, j):
    rho = buf[j, 150:160, :]
    return [rho] + [rho * buf[j, c * 50 : c * 50 + 10, :] for c in range(3)] + [buf[j, 160:170, :]]


def les_rows(buf, j):
    return [buf[j, c * 10 : c * 10 + 10, :] for c in range(5)]


def les_common(ql, qr, k):
    rl, vl, pl_ = les_prims(ql)
    rr, vr, pr = les_prims(qr)
    fl, fr = les_flux(ql, vl, pl_, k), les_flux(qr, vr, pr, k)
    return common(fl, fr, les_speed(rl, vl, pl_, k), les_speed(rr, vr, pr, k), ql, qr), fl, fr


def les_change(own, nbr, k, side):
    ro, vo, po = les_prims(own)
    rn, vn, pn = les_prims(nbr)
    fo, fn = les_flux(own, vo, po, k), les_flux(nbr, vn, pn, k)
    half = 0.5 * LIFT * jnp.maximum(les_speed(ro, vo, po, k), les_speed(rn, vn, pn, k))
    return [(0.5 * LIFT * side) * (fo[n] - fn[n]) + half * (nbr[n] - own[n]) for n in range(5)]


def ape_change(own, nbr, k, side):
    half = 0.5 * LIFT * jnp.maximum(jnp.abs(own[6 + k]) + own[5], jnp.abs(nbr[6 + k]) + nbr[5])
    out = [half * (nbr[n] - own[n]) for n in range(4)]
    out[0] = out[0] + (0.5 * LIFT * side) * (ape_leading(own, k) - ape_leading(nbr, k))
    out[1 + k] = out[1 + k] + (0.5 * LIFT * side) * (ape_carried(own) - ape_carried(nbr))
    return out


def finish_kernel(
    les, ac, acc, da_in, lamb_own, m, pp, back, fwd, inner, outer, axial,
    fwd_in, inner_in, outer_in, axial_in, back_in, perm, perm_t, coef,
    les_out, ac_out, delta, result, yn, rt, rhs, osc, da, corr, sem,
):
    rad = lax.axis_index("rad")
    even = lax.rem(rad, 2) == 0
    first_half = lax.axis_index("group") == 0
    inner_side, axis_side = jnp.where(even, 1.0, -1.0), jnp.where(first_half, 1.0, -1.0)
    inner_row = jnp.where(even, 9, 0)
    at_end = (rad == 0) | (rad == lax.axis_size("rad") - 1)

    def les_faces():
        value = relane(wide(acc), perm_t[...])
        for j in range(5):
            delta[j] = value[:, tile(j)]
        for j in range(5):

            def add(start, stride, change):
                for n in range(5):
                    at = pl.ds(n * 100 + start, 10, stride=stride)
                    delta[j, at, :] = delta[j, at, :] + change[n]

            add(inner_row, 10, les_change(les_rows(inner, j), les_rows(inner_in, j), 1, inner_side))
            own = les_rows(outer, j)
            nbr = [jnp.where(at_end, o, n) for o, n in zip(own, les_rows(outer_in, j))]
            add(9 - inner_row, 10, les_change(own, nbr, 1, -inner_side))
            add(0, 1, les_change(back_face(back, j), les_rows(fwd_in, j), 0, -1.0))
            add(90, 1, les_change(les_rows(fwd, j), back_face(back_in, j), 0, 1.0))
        own = [axial[16 * c : 16 * c + 16, :] for c in range(5)]
        nbr = [axial_in[16 * c : 16 * c + 16, :] for c in range(5)]
        change = les_change(own, nbr, 2, axis_side)
        lane = lax.broadcasted_iota(jnp.int32, (10, 128), 1)
        on_last = (lane == 127) & first_half
        on_first = (lane == 0) & jnp.logical_not(first_half)
        for n in range(5):
            for a in range(10):
                column = jnp.broadcast_to(change[n][0:10, a : a + 1], (10, 128))
                at = slice(n * 100 + a * 10, n * 100 + a * 10 + 10)
                for j in range(5):
                    value = delta[j, at, :]
                    if j == 0:
                        value = value + jnp.where(on_first, column, 0.0)
                    if j == 4:
                        value = value + jnp.where(on_last, column, 0.0)
                    result[n, a, :, tile(j)] = les[n, a, :, tile(j)] + DT * value

    def send_les():
        pltpu.make_async_copy(result, les_out, sem).start()

    def sources():
        value = relane(jnp.concatenate([back_in[j, 0:160, :] for j in range(5)], axis=1), perm[...])
        for j in range(5):
            yn[j] = value[:, tile(j)]
        for c in range(3):
            for i in range(2):
                rt[i, c * 128 + 120 : c * 128 + 128, :] = jnp.zeros((8, 128), F32)
        dcoefs = [coef[2, k] for k in range(5)]
        for er in range(2):
            v = [[[None] * 5 for _ in range(5)] for _ in range(3)]
            for c in range(3):
                for a in range(5):
                    at = c * 50 + a * 10 + er * 5
                    v[c][a] = [yn[j, at : at + 8, :] for j in range(5)]
            d2v0 = [apply5(v[0][a], D) for a in range(5)]
            d2v1 = [apply5(v[1][a], D) for a in range(5)]
            for j in range(5):
                d0v1 = apply5([v[1][a][j] for a in range(5)], D)
                d0v2 = apply5([v[2][a][j] for a in range(5)], D)
                for a in range(5):
                    w0 = radial(v[2][a][j], dcoefs) - d2v1[a][j]
                    w1 = d2v0[a][j] - d0v2[a]
                    w2 = d0v1[a] - radial(v[0][a][j], dcoefs)
                    lamb = [
                        w1 * v[2][a][j] - w2 * v[1][a][j],
                        w2 * v[0][a][j] - w0 * v[2][a][j],
                        w0 * v[1][a][j] - w1 * v[0][a][j],
                    ]
                    for c in range(3):
                        rt[er, pl.ds(c * 128 + a * 25 + j, 5, stride=5), :] = lamb[c][0:5]
        near = jnp.concatenate(split(wide(rt)), axis=0)
        s = dot(jnp.concatenate([lamb_own[...], near], axis=1), m[...])
        s = s[0:384] + s[384:768]
        for p in range(8):
            for c in range(3):
                hi, lo = split(s[c * 128 : c * 128 + 128, tile(p)])
                rhs[p * 128 : p * 128 + 128, tile(c)] = hi
                rhs[1024 + p * 128 : 1152 + p * 128, tile(c)] = hi
                rhs[2048 + p * 128 : 2176 + p * 128, tile(c)] = lo
        out = dot(pp[...], rhs[...])
        for c in range(3):
            osc[c] = out[:, tile(c)]

    axial_change = []

    def acoustic_faces():
        for j in range(5):
            corr[j] = jnp.zeros((104, 128), F32)

            def add(start, stride, change):
                for n in range(4):
                    at = pl.ds(start + n, 5, stride=stride)
                    corr[j, at, :] = corr[j, at, :] + change[n]

            add(0, 4, ape_change(ape_face(back, B_APE, j), ape_face(fwd_in, F_APE, j), 0, -1.0))
            add(80, 4, ape_change(ape_face(fwd, F_APE, j), ape_face(back_in, B_APE, j), 0, 1.0))
            own, nbr = ape_face(inner, F_APE, j), ape_face(inner_in, F_APE, j)
            add(jnp.where(even, 16, 0), 20, ape_change(own, nbr, 1, inner_side))
            own = ape_face(outer, F_APE, j)
            nbr = [jnp.where(at_end, o, n) for o, n in zip(own, ape_face(outer_in, F_APE, j))]
            add(jnp.where(even, 0, 16), 20, ape_change(own, nbr, 1, -inner_side))

        def axial_state(buf):
            def spread(base):
                rows = buf[base : base + 8, :]
                row = lax.broadcasted_iota(jnp.int32, (8, 128), 0)
                lanes = lax.broadcasted_iota(jnp.int32, (8, 128), 1)
                out = jnp.zeros((8, 128), F32)
                for a in range(5):
                    here = (lanes == a * 5 + row) & (row < 5)
                    out = jnp.where(here, jnp.broadcast_to(rows[:, a : a + 1], (8, 128)), out)
                return jnp.sum(out, axis=0, keepdims=True)

            used = lax.broadcasted_iota(jnp.int32, (1, 128), 1) < 25
            return (
                [buf[80 + c : 81 + c, :] for c in range(4)]
                + [jnp.where(used, spread(88), 1.0), spread(96)]
                + [buf[84 + k : 85 + k, :] for k in range(3)]
            )

        own, nbr = axial_state(axial), axial_state(axial_in)
        axis = jnp.concatenate(ape_change(own, nbr, 2, axis_side), axis=0)
        axial_change.append(axis)

    def acoustic():
        for j in range(5):
            da[j] = da_in[j]
            for a in range(5):
                for n in range(1, 4):
                    at = pl.ds(a * 20 + n, 5, stride=4)
                    da[j, at, :] = da[j, at, :] - osc[n - 1, pl.ds(a * 25 + j, 5, stride=5), :]
        value = relane(wide(da), perm_t[...])

        axis = axial_change[0]
        lane4 = lax.broadcasted_iota(jnp.int32, (4, 128), 1)
        on_last = (lane4 == 127) & first_half
        on_first = (lane4 == 0) & jnp.logical_not(first_half)
        for j in range(5):
            da[j] = value[:, tile(j)] + corr[j]

            for a in range(5):
                for r in range(5):
                    i = a * 5 + r
                    change = da[j, 4 * i : 4 * i + 4, :]
                    if j == 0 or j == 4:
                        column = jnp.broadcast_to(axis[:, i : i + 1], (4, 128))
                        change = change + jnp.where(on_last if j == 4 else on_first, column, 0.0)
                    ac_out[a, r, :, tile(j)] = ac[a, r, :, tile(j)] + DT * change

    for part in (les_faces, send_les, sources, acoustic_faces, acoustic):
        part()
    pltpu.make_async_copy(result, les_out, sem).wait()


def shape(*dims, dtype=F32):
    return jax.ShapeDtypeStruct(dims, dtype)


def cost(flops, size):
    return pl.CostEstimate(flops=flops, bytes_accessed=size, transcendentals=0)


def params():
    return pltpu.CompilerParams(vmem_limit_bytes=VMEM_LIMIT)


def body(les, ac, den, snd, mv, proj, counts, elem, pattern):
    vmem = pl.BlockSpec(memory_space=pltpu.VMEM)
    ac = jnp.transpose(ac, (1, 2, 0, 3))
    mv = jnp.transpose(mv, (1, 2, 0, 3))
    proj = jnp.transpose(proj, (1, 0, 2)).reshape(1000, 125)
    counts, elem, pattern = counts.reshape(1, 128), elem.reshape(1, 768), pattern.reshape(1, 768)
    perm = jnp.asarray(np.tile(lane_split(), (2, 1)), BF16)
    perm_t = jnp.asarray(np.tile(lane_split().T, (2, 1)), BF16)
    coef = jnp.asarray(radial_coefs(), F32)

    hbm = pl.BlockSpec(memory_space=pltpu.HBM)
    held = [pltpu.VMEM(a.shape, F32) for a in (les, ac, den, snd, mv)]
    back, fwd, inner, outer, axial, les, ac, den, snd, mv = pl.pallas_call(
        pack_kernel,
        out_shape=[pltpu.VMEM((5, n, 128), F32) for n in (B_ROWS, F_ROWS, F_ROWS, F_ROWS)]
        + [pltpu.VMEM((G_ROWS, 128), F32)]
        + held,
        in_specs=[hbm] * 5,
        out_specs=[vmem] * 10,
        scratch_shapes=[pltpu.SemaphoreType.DMA((14,))],
        compiler_params=params(),
        cost_estimate=cost(1_000_000, 5_000_000),
        name="pack",
    )(*[pltpu.with_memory_space_constraint(a, pltpu.HBM) for a in (les, ac, den, snd, mv)])

    azim, radc = lax.axis_size("azim"), lax.axis_size("rad")
    back_in = lax.ppermute(back, "azim", [(i, (i - 1) % azim) for i in range(azim)])
    fwd_in = lax.ppermute(fwd, "azim", [(i, (i + 1) % azim) for i in range(azim)])
    inner_in = lax.ppermute(inner, "rad", [(i, i ^ 1) for i in range(radc)])
    outer_in = lax.ppermute(outer, "rad", [p for i in range(1, radc - 1, 2) for p in ((i, i + 1), (i + 1, i))])
    axial_in = lax.ppermute(axial, "group", [(0, 1), (1, 0)])

    acc, da, lamb, m, pp = pl.pallas_call(
        interior_kernel,
        out_shape=[
            shape(5, 512, 128), shape(5, 104, 128), shape(768, 512, dtype=BF16), shape(768, 1024, dtype=BF16),
            shape(128, 3072, dtype=BF16),
        ],
        in_specs=[vmem] * 11,
        out_specs=[vmem] * 5,
        scratch_shapes=[
            pltpu.VMEM((5, ROWS, 128), F32),
            pltpu.VMEM((5, ROWS, 128), F32),
            pltpu.VMEM((4, 5, 160, 128), F32),
            pltpu.VMEM((3, 5, 160, 128), F32),
            pltpu.VMEM((4, 384, 128), F32),
            pltpu.VMEM((768, 768), BF16),
            pltpu.VMEM((1024, 768), BF16),
            pltpu.VMEM((1024, 128), F32),
        ],
        compiler_params=params(),
        cost_estimate=cost(5_000_000_000, 10_000_000),
        name="interior",
    )(les, ac, den, snd, mv, proj, counts, elem, pattern, perm, coef)

    les_next, ac_next = pl.pallas_call(
        finish_kernel,
        out_shape=[shape(5, 10, 10, NX), shape(5, 5, 4, NX)],
        in_specs=[vmem] * 20,
        out_specs=[hbm, vmem],
        scratch_shapes=[
            pltpu.VMEM((5, 512, 128), F32),
            pltpu.VMEM((5, 10, 10, NX), F32),
            pltpu.VMEM((5, 160, 128), F32),
            pltpu.VMEM((2, 384, 128), F32),
            pltpu.VMEM((3072, 384), BF16),
            pltpu.VMEM((3, 128, 128), F32),
            pltpu.VMEM((5, 104, 128), F32),
            pltpu.VMEM((5, 104, 128), F32),
            pltpu.SemaphoreType.DMA(()),
        ],
        compiler_params=params(),
        cost_estimate=cost(500_000_000, 4_000_000),
        name="finish",
    )(
        les, ac, acc, da, lamb, m, pp, back, fwd, inner, outer, axial,
        fwd_in, inner_in, outer_in, axial_in, back_in, perm, perm_t, coef,
    )
    return les_next, jnp.transpose(ac_next, (2, 0, 1, 3))


def solution(mesh):
    field = P(None, "azim", "rad", "group")
    node = P("azim", "rad", "group")
    lists = P("azim", "rad", "group", None)
    return jax.shard_map(
        body,
        mesh=mesh,
        in_specs=(field, field, node, node, field, P(), lists, lists, lists),
        out_specs=(field, field),
        check_vma=False,
    )
```
